128 devices in a mesh: lon: 8 (over y, core), lat: 16 (over z, x).
Axes of the slice: x: 4, y: 4, z: 4, core: 2. Of those that a mesh axis runs over, the one named last changes fastest.
Arguments:
- prior_state: float32 [80, 128, 256, 128], P(None, 'lon', 'lat'), may hold values from -6 to 6
- stencil: int32 [2, 8, 16, 32, 4], P(None, 'lon', 'lat'), may hold values from 0 to 4194303, as said below
- weights: float32 [2, 8, 16, 32, 4], P(None, 'lon', 'lat'), may hold values from 0.2 to 1
- obs_values: float32 [2, 8, 16, 32], P(None, 'lon', 'lat'), may hold values from -8 to 8
- obs_errors: float32 [2, 8, 16, 32], P(None, 'lon', 'lat'), may hold values from 0.25 to 4
- radius: int32 [2, 8, 16, 32], P(None, 'lon', 'lat'), may hold values from 1 to 16, as said below
Outputs:
- posterior_state: float32 [80, 128, 256, 128], P(None, 'lon', 'lat')
- prior_means: float32 [2, 8, 16, 32], P(None, 'lon', 'lat')
The draws below stay inside these ranges and needn't reach their ends.
Inputs may be any that keep to these rules, and one draw needn't show every extreme that they name: The first stencil row of an observation lies in a block owned by the observation's owner, block ((owner along lon) * 16 + i, (owner along lat) * 16 + j) with 0 <= i, j < 16; every other stencil row lies in a block at most one block away along each dimension, inside the grid. Both the first and the last row of the grid occur. Each device owns at least one observation with the largest radius in each batch.
All inputs are finite; a program needn't handle non-finite values.
Results may differ from the reference program's by a relative error of at most 0.0003.
Values sent between devices are 32-bit elements; how exact they have to be, the bound alone decides.
No kernel may reach another device: no remote copies, remote signals or barrier semaphores. Data moves between devices by JAX's collectives and lax.ppermute only.
A program may use at most 192 MiB of HBM per device.

```python
import math
import jax
import jax.numpy as jnp
from jax import lax

MEMBERS = 80
BLOCK = 128
BLK_SIDE = 16
OBS_DEV = 32
STENCIL = 4
BATCHES = 2
RADIUS = 16
NLONB = 128
NLATB = 256
OLON = 8
OLAT = 16


def draw_stencil(key, part):
    key = jax.random.fold_in(key, 11)
    keys = jax.random.split(key, 5)
    shape = (BATCHES, OLON, OLAT, OBS_DEV)
    lon_owner = lax.broadcasted_iota(jnp.int32, shape, 1)
    lat_owner = lax.broadcasted_iota(jnp.int32, shape, 2)
    first_lon = lon_owner * BLK_SIDE + jax.random.randint(keys[0], shape, 0, BLK_SIDE)
    first_lat = lat_owner * BLK_SIDE + jax.random.randint(keys[1], shape, 0, BLK_SIDE)
    first_lon = first_lon.at[0, 0, 0, 0].set(0).at[0, OLON - 1, OLAT - 1, 0].set(NLONB - 1)
    first_lat = first_lat.at[0, 0, 0, 0].set(0).at[0, OLON - 1, OLAT - 1, 0].set(NLATB - 1)
    full = shape + (STENCIL,)
    offset_lon = jax.random.randint(keys[2], full, -1, 2).at[..., 0].set(0)
    offset_lat = jax.random.randint(keys[3], full, -1, 2).at[..., 0].set(0)
    block_lon = jnp.clip(first_lon[..., None] + offset_lon, 0, NLONB - 1)
    block_lat = jnp.clip(first_lat[..., None] + offset_lat, 0, NLATB - 1)
    cell_index = jax.random.randint(keys[4], full, 0, BLOCK)
    cell_index = cell_index.at[0, 0, 0, 0, 0].set(0).at[0, OLON - 1, OLAT - 1, 0, 0].set(BLOCK - 1)
    return ((block_lon * NLATB + block_lat) * BLOCK + cell_index).astype(jnp.int32)


def draw_radius(key, part):
    key = jax.random.fold_in(key, 23)
    shape = (BATCHES, OLON, OLAT, OBS_DEV)
    values = jax.random.randint(key, shape, 1, RADIUS + 1)
    return values.at[..., 0].set(RADIUS).astype(jnp.int32)


def block_scale(own_key, extent, pieces, low, high):
    gain, own = 1.0, jax.random.fold_in(own_key, 6)
    for dim, shards_of in pieces:
        draws = jnp.exp(jax.random.uniform(jax.random.fold_in(own, dim), (shards_of,), jnp.float32, low / len(pieces), high / len(pieces)))
        gain = gain * jnp.repeat(draws, extent[dim] // shards_of).reshape([-1 if axis == dim else 1 for axis in range(len(extent))])
    return gain


def scatter_about(stream_key, shape, scale, most, cuts=(), held_as=jnp.bfloat16):
    level = block_scale(stream_key, shape, cuts, -0.22, 0.18) if cuts else 1.0
    drawn = jax.random.normal(stream_key, shape, jnp.float32) * scale * level
    return jnp.minimum(jnp.maximum(drawn, -most), most).astype(held_as)


def setup_inputs(seed: int = 0) -> dict:
    splits = jax.random.split(jax.random.key(seed), 7)
    prior_state = scatter_about(splits[0], (MEMBERS, NLONB, NLATB, BLOCK), 1.0, 6.0, ((1, 8), (2, 16)), jnp.float32)
    stencil = draw_stencil(jax.random.fold_in(splits[6], 71), 0)
    weights = jnp.clip(0.2 + 0.8 * jax.random.uniform(splits[2], (BATCHES, OLON, OLAT, OBS_DEV, STENCIL), jnp.float32) ** block_scale(splits[2], (BATCHES, OLON, OLAT, OBS_DEV, STENCIL), ((1, 8), (2, 16)), -0.2, 0.2), 0.2, 1.0)
    obs_values = scatter_about(splits[3], (BATCHES, OLON, OLAT, OBS_DEV), 1.5, 8.0, ((1, 8), (2, 16)), jnp.float32)
    obs_errors = jnp.clip(jnp.exp(math.log(4.0) - 2.7725887 * jax.random.uniform(splits[4], (BATCHES, OLON, OLAT, OBS_DEV), jnp.float32) ** block_scale(splits[4], (BATCHES, OLON, OLAT, OBS_DEV), ((1, 8), (2, 16)), -0.2, 0.2)), 0.25, 4.0)
    radius = draw_radius(jax.random.fold_in(splits[6], 71), 0)
    return dict(prior_state=prior_state, stencil=stencil, weights=weights, obs_values=obs_values, obs_errors=obs_errors, radius=radius)


EPS = 1e-06
HIGH = lax.Precision.HIGHEST

def observe(state_flat, stencil_rows, stencil_weights, values, errors):
    ensemble = jnp.zeros(stencil_rows.shape[:-1] + (MEMBERS,), jnp.float32)
    for point in range(STENCIL):
        picked = jnp.moveaxis(state_flat[:, stencil_rows[..., point]], 0, -1)
        ensemble = ensemble + stencil_weights[..., point][..., None] * picked
    prior_mean = lax.optimization_barrier(jnp.mean(ensemble, axis=-1))
    anomaly = ensemble - prior_mean[..., None]
    spread = lax.optimization_barrier(jnp.sum(anomaly * anomaly, axis=-1)) / (MEMBERS - 1) + EPS
    post_var = 1.0 / (1.0 / spread + 1.0 / errors)
    post_mean = post_var * (prior_mean / spread + values / errors)
    obs_delta = (post_mean - prior_mean)[..., None] + (jnp.sqrt(post_var / spread) - 1.0)[..., None] * anomaly
    obs_gain = anomaly / ((MEMBERS - 1) * spread)[..., None]
    return (jnp.stack([obs_gain, obs_delta], axis=-2), prior_mean)

def regress(region, near_pack, near_meta, lon_index, lat_index):
    members = region.shape[0]
    side = region.shape[1]
    cells = region.shape[3]
    anomal = region - lax.optimization_barrier(jnp.mean(region, axis=0, keepdims=True))
    obs_gain = near_pack[:, 0, :]
    obs_delta = near_pack[:, 1, :]
    obs_lon = near_meta[:, 0]
    obs_lat = near_meta[:, 1]
    reach = (near_meta[:, 2] + 1).astype(jnp.float32)
    lat_blocks = lat_index * side + jnp.arange(side, dtype=jnp.int32)
    lat_gap = jnp.abs(lat_blocks[:, None] - obs_lat[None, :])

    def lon_block(column):
        lon_gap = jnp.abs(lon_index * side + column - obs_lon)
        distance = jnp.maximum(lon_gap[None, :], lat_gap)
        taper = jnp.maximum(0.0, 1.0 - distance.astype(jnp.float32) / reach[None, :])
        strip = anomal[:, column].reshape(members, side * cells)
        covariance = lax.dot_general(strip, obs_gain, (((0,), (1,)), ((), ())), precision=HIGH)
        regressed = (covariance.reshape(side, cells, -1) * taper[:, None, :]).reshape(side * cells, -1)
        change = lax.dot_general(obs_delta, regressed, (((0,), (1,)), ((), ())), precision=HIGH)
        return region[:, column].reshape(members, side * cells) + change
    updated = lax.map(lon_block, jnp.arange(side, dtype=jnp.int32))
    return jnp.moveaxis(updated, 0, 1).reshape(region.shape)

def reference(prior_state, stencil, weights, obs_values, obs_errors, radius):
    state = prior_state
    means_list = []
    zero_index = jnp.zeros((), jnp.int32)
    for batch in range(BATCHES):
        obs_pack, prior_mean = observe(state.reshape(MEMBERS, -1), stencil[batch], weights[batch], obs_values[batch], obs_errors[batch])
        first_row = stencil[batch][..., 0]
        obs_meta = jnp.stack([first_row // (NLATB * BLOCK), first_row // BLOCK % NLATB, radius[batch]], axis=-1).astype(jnp.int32)
        pack_pad = jnp.pad(obs_pack, ((1, 1), (1, 1), (0, 0), (0, 0), (0, 0)))
        meta_pad = jnp.pad(obs_meta, ((1, 1), (1, 1), (0, 0), (0, 0)))

        def device_region(flat_index):
            lon_index = (flat_index // OLAT).astype(jnp.int32)
            lat_index = (flat_index % OLAT).astype(jnp.int32)
            lon_start = (lon_index * BLK_SIDE).astype(jnp.int32)
            lat_start = (lat_index * BLK_SIDE).astype(jnp.int32)
            region = lax.dynamic_slice(state, (zero_index, lon_start, lat_start, zero_index), (MEMBERS, BLK_SIDE, BLK_SIDE, BLOCK))
            near_pack = lax.dynamic_slice(pack_pad, (lon_index, lat_index, zero_index, zero_index, zero_index), (3, 3, OBS_DEV, 2, MEMBERS)).reshape(9 * OBS_DEV, 2, MEMBERS)
            near_meta = lax.dynamic_slice(meta_pad, (lon_index, lat_index, zero_index, zero_index), (3, 3, OBS_DEV, 3)).reshape(9 * OBS_DEV, 3)
            return regress(region, near_pack, near_meta, lon_index, lat_index)
        regions = lax.map(device_region, jnp.arange(OLON * OLAT, dtype=jnp.int32))
        regions = regions.reshape(OLON, OLAT, MEMBERS, BLK_SIDE, BLK_SIDE, BLOCK)
        state = jnp.transpose(regions, (2, 0, 3, 1, 4, 5)).reshape(MEMBERS, NLONB, NLATB, BLOCK)
        means_list.append(prior_mean)
    return (state, jnp.stack(means_list))
```

```python
import functools
import jax
import jax.numpy as jnp
from jax import lax
from jax.experimental import pallas as pl
from jax.experimental.pallas import tpu as pltpu
from jax.sharding import PartitionSpec as P

EPS = 1e-06
LANES = 128
F32 = jnp.float32
BF16 = jnp.bfloat16


def neighbours(array, axis):
    size = lax.axis_size(axis)
    up = [(i, i + 1) for i in range(size - 1)]
    down = [(j, i) for i, j in up]
    return lax.ppermute(array, axis, up), lax.ppermute(array, axis, down)


def split(x):
    high = x.astype(BF16)
    return high, (x - high.astype(F32)).astype(BF16)


def pick_kernel(obs, points, code_ref, loc_ref, w_ref, state_ref, before_ref, own_ref, after_ref):
    outs = (before_ref, own_ref, after_ref)
    members = own_ref.shape[0]
    blocks = state_ref.shape[0] // members
    lane = lax.broadcasted_iota(jnp.int32, (members, LANES), 1)
    for out in outs:
        out[...] = jnp.zeros_like(out)

    def one(group, out, slot, o):
        acc = jnp.zeros((members, LANES), F32)
        for s in range(points):
            at = (group * obs + o) * points + s
            loc = loc_ref[at]
            w = jnp.where(loc >= 0, w_ref[at], 0.0)
            loc = jnp.maximum(loc, 0)
            x = state_ref[pl.ds(loc // LANES, members, stride=blocks), :]
            acc = acc + jnp.where(lane == loc % LANES, x * w, 0.0)
        total = jnp.sum(acc, axis=1, keepdims=True)
        out[...] += jnp.where(lane == slot * obs + o, total, 0.0)

    for i in range(3):
        for j in range(3):
            group = i * 3 + j

            @pl.loop(0, obs)
            def _(o, group=group, out=outs[j], slot=i):
                @pl.when(code_ref[group * obs + o] > 0)
                def _():
                    one(group, out, slot, o)


def pick(code, loc, w, state, obs, points):
    members, blocks, cells = state.shape
    rows = jax.ShapeDtypeStruct((members, LANES), F32)
    smem = pl.BlockSpec(memory_space=pltpu.SMEM)
    vmem = pl.BlockSpec(memory_space=pltpu.VMEM)
    return pl.pallas_call(
        functools.partial(pick_kernel, obs, points),
        out_shape=(rows,) * 3,
        in_specs=[smem, smem, smem, vmem],
        out_specs=(vmem,) * 3,
        compiler_params=pltpu.CompilerParams(vmem_limit_bytes=40 * 1024 * 1024),
    )(code, loc, w, state.reshape(members * blocks, cells))


def observe_kernel(obs, slot_ref, before_ref, own_ref, after_ref, about_ref, pack_ref, mean_ref):
    members = own_ref.shape[0]
    lane = lax.broadcasted_iota(jnp.int32, (1, LANES), 1)
    mine = lane < obs
    ensemble = (
        pltpu.roll(own_ref[...], LANES - obs, 1)
        + pltpu.roll(before_ref[...], LANES - 2 * obs, 1)
        + after_ref[...]
    )
    ensemble = jnp.where(mine, ensemble, 0.0)
    values = about_ref[0:1, :]
    errors = jnp.where(mine, about_ref[1:2, :], 1.0)
    mean = jnp.sum(ensemble, axis=0, keepdims=True) / members
    anomaly = ensemble - mean
    spread = jnp.sum(anomaly * anomaly, axis=0, keepdims=True) / (members - 1) + EPS
    post_var = 1.0 / (1.0 / spread + 1.0 / errors)
    post_mean = post_var * (mean / spread + values / errors)
    delta = (post_mean - mean) + (jnp.sqrt(post_var / spread) - 1.0) * anomaly
    gain = anomaly / ((members - 1) * spread)
    shift = slot_ref[0] * obs
    pack_ref[0:members, :] = pltpu.roll(jnp.where(mine, gain, 0.0), shift, 1)
    pack_ref[members : 2 * members, :] = pltpu.roll(jnp.where(mine, delta, 0.0), shift, 1)
    pack_ref[2 * members :, :] = pltpu.roll(jnp.where(mine, about_ref[...], 0.0), shift, 1)
    mean_ref[...] = jnp.broadcast_to(mean, mean_ref.shape)


def observe(slot, before, own, after, about, obs):
    members = own.shape[0]
    smem = pl.BlockSpec(memory_space=pltpu.SMEM)
    vmem = pl.BlockSpec(memory_space=pltpu.VMEM)
    return pl.pallas_call(
        functools.partial(observe_kernel, obs),
        out_shape=(
            jax.ShapeDtypeStruct((2 * members + 8, LANES), F32),
            jax.ShapeDtypeStruct((8, LANES), F32),
        ),
        in_specs=[smem, vmem, vmem, vmem, vmem],
        out_specs=(vmem, vmem),
    )(slot, before, own, after, about)


def update_kernel(pos_ref, c0_ref, c1_ref, c2_ref, state_ref, out_ref, w_ref, lhs_ref, a_ref):
    chunks = (c0_ref, c1_ref, c2_ref)
    members, side, cells = state_ref.shape
    column = pl.program_id(0)

    @pl.when(column == 0)
    def _():
        for j, c in enumerate(chunks):
            gain = jnp.concatenate([c[0:members, :], jnp.zeros((LANES - members, LANES), F32)], axis=0)
            high, low = split(gain.T)
            both = jnp.concatenate([high, low], axis=1)
            w_ref[pl.ds(j * 2 * LANES, LANES), :] = both
            w_ref[pl.ds(j * 2 * LANES + LANES, LANES), :] = both

    lon = (pos_ref[0] * side + column).astype(F32)
    lat = (pos_ref[1] * side + lax.broadcasted_iota(jnp.int32, (side, 1), 0)).astype(F32)
    for j, c in enumerate(chunks):
        about = c[2 * members : 2 * members + 8, :]
        reach = about[4:5, :]
        gap = jnp.maximum(jnp.abs(lon - about[2:3, :]), jnp.abs(lat - about[3:4, :]))
        taper = jnp.maximum(0.0, reach - gap) / jnp.maximum(reach, 1.0)
        delta = c[members : 2 * members, :]
        for q in range(side):
            high, low = split(delta * taper[q : q + 1, :])
            lhs_ref[q * members : (q + 1) * members, j * 2 * LANES : j * 2 * LANES + LANES] = high
            lhs_ref[q * members : (q + 1) * members, j * 2 * LANES + LANES : (j + 1) * 2 * LANES] = low
    a_ref[...] = jnp.dot(lhs_ref[...], w_ref[...], preferred_element_type=F32)
    flat = state_ref.reshape(members * side, cells)
    flat_out = out_ref.reshape(members * side, cells)
    for q in range(side):
        a = a_ref[q * members : (q + 1) * members, 0:LANES] + a_ref[q * members : (q + 1) * members, LANES:]
        high, low = split(a)
        x = flat[pl.ds(q, members, stride=side), :]
        xa = x - jnp.sum(x, axis=0, keepdims=True) / members
        x_high, x_low = split(xa)
        left = jnp.concatenate([high[:, :members], high[:, :members], low[:, :members]], axis=1)
        right = jnp.concatenate([x_high, x_low, x_high], axis=0)
        flat_out[pl.ds(q, members, stride=side), :] = x + jnp.dot(left, right, preferred_element_type=F32)


def update(pos, chunks, state, side):
    members, blocks, cells = state.shape
    vmem = pl.BlockSpec(memory_space=pltpu.VMEM)
    strip = pl.BlockSpec((members, side, cells), lambda p: (0, p, 0))
    return pl.pallas_call(
        update_kernel,
        grid=(blocks // side,),
        out_shape=jax.ShapeDtypeStruct(state.shape, F32),
        in_specs=[pl.BlockSpec(memory_space=pltpu.SMEM), vmem, vmem, vmem, strip],
        out_specs=strip,
        scratch_shapes=[
            pltpu.VMEM((3 * 2 * LANES, 2 * LANES), BF16),
            pltpu.VMEM((side * members, 3 * 2 * LANES), BF16),
            pltpu.VMEM((side * members, 2 * LANES), F32),
        ],
        compiler_params=pltpu.CompilerParams(vmem_limit_bytes=40 * 1024 * 1024),
    )(pos, *chunks, state)


def per_device(prior_state, stencil, weights, obs_values, obs_errors, radius):
    members, side, _, cells = prior_state.shape
    batches, _, _, obs, points = stencil.shape
    lon_index = lax.axis_index("lon")
    lat_index = lax.axis_index("lat")
    lat_total = side * lax.axis_size("lat")
    state = prior_state.reshape(members, side * side, cells)

    own_meta = jnp.concatenate(
        [stencil.reshape(batches, obs * points).astype(F32) + 1.0, weights.reshape(batches, obs * points)]
    )
    before, after = neighbours(own_meta, "lat")
    row_meta = jnp.stack([before, own_meta, after])
    before, after = neighbours(row_meta, "lon")
    meta = jnp.stack([before, row_meta, after]).reshape(9, 2, batches, obs * points)
    rows = meta[:, 0].astype(jnp.int32) - 1
    block_lon = rows // (lat_total * cells) - lon_index * side
    block_lat = rows // cells % lat_total - lat_index * side
    here = (rows >= 0) & (block_lon >= 0) & (block_lon < side) & (block_lat >= 0) & (block_lat < side)
    loc = jnp.where(here, (block_lon * side + block_lat) * cells + rows % cells, -1)
    code = jnp.max(here.astype(jnp.int32).reshape(9, batches, obs, points), axis=-1)
    loc = jnp.moveaxis(loc, 1, 0).reshape(batches, -1)
    code = jnp.moveaxis(code, 1, 0).reshape(batches, -1)
    w = jnp.moveaxis(meta[:, 1], 1, 0).reshape(batches, -1)

    first = stencil[:, 0, 0, :, 0]
    about = jnp.stack(
        [
            obs_values[:, 0, 0],
            obs_errors[:, 0, 0],
            (first // (lat_total * cells)).astype(F32),
            (first // cells % lat_total).astype(F32),
            (radius[:, 0, 0] + 1).astype(F32),
        ],
        axis=1,
    )
    about = jnp.pad(about, ((0, 0), (0, 3), (0, LANES - obs)))
    slot = (lat_index % 4).astype(jnp.int32).reshape(1)
    pos = jnp.stack([lon_index, lat_index]).astype(jnp.int32)

    means = []
    for batch in range(batches):
        to_before, to_own, to_after = pick(code[batch], loc[batch], w[batch], state, obs, points)
        size = lax.axis_size("lat")
        from_before = lax.ppermute(to_after, "lat", [(i, i + 1) for i in range(size - 1)])
        from_after = lax.ppermute(to_before, "lat", [(i + 1, i) for i in range(size - 1)])
        summed = from_before + to_own + from_after
        before, after = neighbours(summed, "lon")
        pack, mean = observe(slot, before, summed, after, about[batch], obs)
        before, after = neighbours(pack, "lat")
        merged = before + pack + after
        before, after = neighbours(merged, "lon")
        state = update(pos, (before, merged, after), state, side)
        means.append(mean[0, :obs])
    return state.reshape(prior_state.shape), jnp.stack(means)[:, None, None, :]


def solution(mesh):
    placed = (
        P(None, "lon", "lat", None),
        P(None, "lon", "lat", None, None),
        P(None, "lon", "lat", None, None),
        P(None, "lon", "lat", None),
        P(None, "lon", "lat", None),
        P(None, "lon", "lat", None),
    )
    return jax.shard_map(
        per_device,
        mesh=mesh,
        in_specs=placed,
        out_specs=(P(None, "lon", "lat", None), P(None, "lon", "lat", None)),
        check_vma=False,
    )
```

```python
import functools
import jax
import jax.numpy as jnp
from jax import lax
from jax.experimental import pallas as pl
from jax.experimental.pallas import tpu as pltpu
from jax.sharding import PartitionSpec as P

EPS = 1e-06
LANES = 128
WORD = 8
F32 = jnp.float32
BF16 = jnp.bfloat16
VMEM_LIMIT = 48 * 1024 * 1024
UNROLL = 4
GROUP = 16


def pitch_of(side):
    return side + 8 if side % 16 == 0 else side


def neighbours(array, axis, distance=1):
    size = lax.axis_size(axis)
    up = [(i, i + distance) for i in range(size - distance)]
    down = [(j, i) for i, j in up]
    return lax.ppermute(array, axis, up), lax.ppermute(array, axis, down)


def split(x):
    high = x.astype(BF16)
    return high, (x - high.astype(F32)).astype(BF16)


def thirds(x):
    high = x.astype(BF16)
    rest = x - high.astype(F32)
    middle = rest.astype(BF16)
    return high, middle, (rest - middle.astype(F32)).astype(BF16)


def pick(obs, points, side, pitch, members, code_ref, loc_ref, w_ref, held, sums):
    lane = lax.broadcasted_iota(jnp.int32, (members, LANES), 1)
    sums[...] = jnp.zeros_like(sums)

    def one(group, o):
        acc = jnp.zeros((members, LANES), F32)
        for s in range(points):
            at = (group * obs + o) * points + s
            loc = loc_ref[at]
            w = jnp.where(loc >= 0, w_ref[at], 0.0)
            loc = jnp.maximum(loc, 0)
            block = loc // LANES
            start = (block // side) * (members * pitch) + block % side
            x = held[pl.ds(start, members, stride=pitch), :]
            acc = acc + jnp.where(lane == loc % LANES, x * w, 0.0)
        total = jnp.sum(acc, axis=1, keepdims=True)
        return jnp.where(lane == (group // 3) * obs + o, total, 0.0)

    @pl.loop(0, obs // UNROLL)
    def _(t):
        found = [one(4, t * UNROLL + u) for u in range(UNROLL)]
        sums[1] = sums[1] + sum(found[1:], found[0])

    per_group = obs // WORD

    @pl.loop(0, 9 * per_group)
    def _(t):
        word = code_ref[t]

        @pl.when((word > 0) & (t // per_group != 4))
        def _():
            @pl.loop(0, WORD)
            def _(k):
                @pl.when((word // (1 << k)) % 2 == 1)
                def _():
                    group = t // per_group
                    sums[group % 3] = sums[group % 3] + one(group, (t % per_group) * WORD + k)


def strips_in(state_ref, st_ref, side, sem):
    return lambda p: pltpu.make_async_copy(
        state_ref.at[:, pl.ds(p * side, side), :], st_ref.at[p, :, pl.ds(0, side), :], sem.at[p]
    )


def pick_kernel(obs, points, code_ref, loc_ref, w_ref, state_ref, before_ref, own_ref, after_ref, st_ref, sums, sem):
    strips, members, pitch, cells = st_ref.shape
    side = state_ref.shape[1] // strips
    copy = strips_in(state_ref, st_ref, side, sem)
    for p in range(strips):
        copy(p).start()
    for p in range(strips):
        copy(p).wait()
    held = st_ref.reshape(strips * members * pitch, cells)
    pick(obs, points, side, pitch, members, code_ref, loc_ref, w_ref, held, sums)
    for j, out in enumerate((before_ref, own_ref, after_ref)):
        out[...] = sums[j]


def first_pick(code, loc, w, state, side, obs, points):
    members, blocks, cells = state.shape
    strips = blocks // side
    rows = jax.ShapeDtypeStruct((members, LANES), F32)
    smem = pl.BlockSpec(memory_space=pltpu.SMEM)
    vmem = pl.BlockSpec(memory_space=pltpu.VMEM)
    return pl.pallas_call(
        functools.partial(pick_kernel, obs, points),
        out_shape=(rows,) * 3,
        in_specs=[smem, smem, smem, pl.BlockSpec(memory_space=pl.ANY)],
        out_specs=(vmem,) * 3,
        scratch_shapes=[
            pltpu.VMEM((strips, members, pitch_of(side), cells), F32),
            pltpu.VMEM((3, members, LANES), F32),
            pltpu.SemaphoreType.DMA((strips,)),
        ],
        compiler_params=pltpu.CompilerParams(vmem_limit_bytes=VMEM_LIMIT),
    )(code, loc, w, state)


def observe_kernel(obs, *refs):
    sums, abouts, (pack_ref, mean_ref) = refs[:5], refs[5:8], refs[8:]
    members = sums[0].shape[0]
    lane = lax.broadcasted_iota(jnp.int32, (1, LANES), 1)

    def placed(x, source, target):
        shift = (target - source) * obs % LANES
        x = x if shift == 0 else pltpu.roll(x, shift, 1)
        return jnp.where((lane >= target * obs) & (lane < (target + 1) * obs), x, 0.0)

    ensemble, about = 0.0, 0.0
    for t in range(3):
        for source in range(3):
            ensemble = ensemble + placed(sums[t + 2 - source][...], source, t)
        about = about + placed(abouts[t][...], 0, t)
    values = about[0:1, :]
    known = about[4:5, :] > 0.0
    errors = jnp.where(known, about[1:2, :], 1.0)
    mean = jnp.sum(ensemble, axis=0, keepdims=True) / members
    anomaly = ensemble - mean
    spread = jnp.sum(anomaly * anomaly, axis=0, keepdims=True) / (members - 1) + EPS
    post_var = 1.0 / (1.0 / spread + 1.0 / errors)
    post_mean = post_var * (mean / spread + values / errors)
    delta = (post_mean - mean) + (jnp.sqrt(post_var / spread) - 1.0) * anomaly
    gain = anomaly / ((members - 1) * spread)
    pack_ref[0:members, :] = jnp.where(known, gain, 0.0)
    pack_ref[members : 2 * members, :] = jnp.where(known, delta, 0.0)
    pack_ref[2 * members :, :] = about
    mean_ref[...] = jnp.broadcast_to(mean, mean_ref.shape)


def observe(sums, abouts, obs):
    members = sums[0].shape[0]
    vmem = pl.BlockSpec(memory_space=pltpu.VMEM)
    return pl.pallas_call(
        functools.partial(observe_kernel, obs),
        out_shape=(
            jax.ShapeDtypeStruct((2 * members + 8, LANES), F32),
            jax.ShapeDtypeStruct((8, LANES), F32),
        ),
        in_specs=[vmem] * 8,
        out_specs=(vmem, vmem),
    )(*sums, *abouts)


def order(about, lon_first, lat_first, side):
    lon, lat, reach = about[2:3, :], about[3:4, :], about[4:5, :]
    lon_gap = jnp.maximum(jnp.maximum(lon_first - lon, lon - (lon_first + side - 1)), 0.0)
    lat_gap = jnp.maximum(jnp.maximum(lat_first - lat, lat - (lat_first + side - 1)), 0.0)
    reached = reach > jnp.maximum(lon_gap, lat_gap)
    cover = jnp.where(lon < lon_first, reach - lon_gap, 2.0 * LANES)
    return jnp.where(reached, cover, -1.0)


def update_kernel(obs, points, *refs):
    if points:
        pos_ref, code_ref, loc_ref, ow_ref, c0_ref, c1_ref, c2_ref, state_ref = refs[:8]
        out_ref, before_ref, own_ref, after_ref, sums = refs[8:12] + refs[-1:]
        st_ref, w_ref, delta_ref, about_ref, a_ref, in_sem, out_sem = refs[12:-1]
    else:
        pos_ref, c0_ref, c1_ref, c2_ref, state_ref, out_ref = refs[:6]
        st_ref, w_ref, delta_ref, about_ref, a_ref, in_sem, out_sem = refs[6:]
    strips, members, pitch, cells = st_ref.shape
    side = state_ref.shape[1] // strips
    rows = members * pitch
    copy_in = strips_in(state_ref, st_ref, side, in_sem)

    def copy_out(p):
        return pltpu.make_async_copy(
            st_ref.at[p, :, pl.ds(0, side), :], out_ref.at[:, pl.ds(p * side, side), :], out_sem.at[p]
        )

    for p in range(strips):
        copy_in(p).start()

    lon_first = (pos_ref[0] * side).astype(F32)
    lat_first = (pos_ref[1] * side).astype(F32)
    near = [
        (c[0:members, :], c[members : 2 * members, :], c[2 * members : 2 * members + 8, :])
        for c in (c0_ref, c1_ref, c2_ref)
    ]
    keys = [order(about, lon_first, lat_first, side) for _, _, about in near]
    lane = lax.broadcasted_iota(jnp.int32, (LANES, LANES), 1)
    sub = lax.broadcasted_iota(jnp.int32, (LANES, LANES), 0)
    picks = []
    for i in range(3):
        mine = jnp.broadcast_to(keys[i], (LANES, LANES)).T
        ahead = jnp.zeros((LANES, LANES), F32)
        for j in range(3):
            before = keys[j] > mine
            if j < i:
                before = before | (keys[j] == mine)
            elif j == i:
                before = before | ((keys[j] == mine) & (lane < sub))
            ahead = ahead + jnp.where(before, 1.0, 0.0)
        rank = jnp.sum(ahead, axis=1, keepdims=True)
        wide = lax.broadcasted_iota(jnp.int32, (LANES, 3 * LANES), 1).astype(F32)
        picks.append(jnp.where(wide == rank, 1.0, 0.0).astype(BF16))
    picks = jnp.concatenate(picks, axis=0)
    gain, delta, about = (jnp.concatenate([n[k] for n in near], axis=1) for k in range(3))
    stack = jnp.concatenate([*thirds(gain), *thirds(delta), about.astype(BF16), jnp.zeros_like(about).astype(BF16)], axis=0)
    moved = jnp.dot(stack, picks, preferred_element_type=F32)
    gain = moved[0:members] + moved[members : 2 * members] + moved[2 * members : 3 * members]
    delta_ref[...] = moved[3 * members : 4 * members] + moved[4 * members : 5 * members] + moved[5 * members : 6 * members]
    about_ref[...] = moved[6 * members : 6 * members + 8]
    for j in range(3):
        part = jnp.concatenate([gain[:, j * LANES : (j + 1) * LANES], jnp.zeros((LANES - members, LANES), F32)], axis=0)
        high, low = split(part.T)
        both = jnp.concatenate([high, low], axis=1)
        w_ref[j, 0:LANES, :] = both
        w_ref[j, LANES:, :] = both

    held = st_ref.reshape(strips * rows, cells)
    lat = lat_first + lax.broadcasted_iota(jnp.int32, (side, 1), 0).astype(F32)

    @pl.loop(0, strips)
    def _(p):
        lon_here = lon_first + p.astype(F32)
        tapers = []
        for j in range(3):
            facts = about_ref[:, j * LANES : (j + 1) * LANES]
            reach = facts[4:5, :]
            gap = jnp.maximum(jnp.abs(lon_here - facts[2:3, :]), jnp.abs(lat - facts[3:4, :]))
            tapers.append(jnp.maximum(0.0, reach - gap) / jnp.maximum(reach, 1.0))

        def matrices(j, first, count):
            delta = delta_ref[:, j * LANES : (j + 1) * LANES]
            left = [jnp.concatenate(split(delta * tapers[j][q : q + 1, :]), axis=1) for q in range(first, first + count)]
            both = jnp.dot(jnp.concatenate(left, axis=0), w_ref[j], preferred_element_type=F32)
            return both[:, :LANES] + both[:, LANES:]

        def finish(more):
            for first in range(0, side, GROUP):
                part = pl.ds(first * members, GROUP * members)
                a = matrices(0, first, GROUP)
                high, low = split(a + a_ref[part, :] if more else a)
                left = jnp.concatenate([high[:, :members], high[:, :members], low[:, :members]], axis=1)
                for q in range(0, GROUP, 2):
                    at = [pl.ds(p * rows + first + q + k, members, stride=pitch) for k in range(2)]
                    x = jnp.concatenate([held[at[0], :], held[at[1], :]], axis=1)
                    x_high, x_low = split(x - jnp.sum(x, axis=0, keepdims=True) / members)
                    right = jnp.concatenate([x_high, x_low, x_high], axis=0)
                    change = jnp.dot(left[q * members : (q + 2) * members], right, preferred_element_type=F32)
                    held[at[0], :] = x[:, :cells] + change[:members, :cells]
                    held[at[1], :] = x[:, cells:] + change[members:, cells:]

        far = jnp.max(jnp.maximum(tapers[1], tapers[2])) > 0.0
        copy_in(p).wait()

        @pl.when(far)
        def _():
            for first in range(0, side, GROUP):
                a_ref[pl.ds(first * members, GROUP * members), :] = matrices(1, first, GROUP)

            @pl.when(jnp.max(tapers[2]) > 0.0)
            def _():
                for first in range(0, side, GROUP):
                    a_ref[pl.ds(first * members, GROUP * members), :] += matrices(2, first, GROUP)

            finish(True)

        @pl.when(jnp.logical_not(far))
        def _():
            finish(False)

        copy_out(p).start()

    if points:
        pick(obs, points, side, pitch, members, code_ref, loc_ref, ow_ref, held, sums)
        for j, out in enumerate((before_ref, own_ref, after_ref)):
            out[...] = sums[j]
    for p in range(strips):
        copy_out(p).wait()


def update(pos, chunks, state, side, obs, following=()):
    members, blocks, cells = state.shape
    strips = blocks // side
    smem = pl.BlockSpec(memory_space=pltpu.SMEM)
    vmem = pl.BlockSpec(memory_space=pltpu.VMEM)
    hbm = pl.BlockSpec(memory_space=pl.ANY)
    rows = jax.ShapeDtypeStruct((members, LANES), F32)
    more = 3 if following else 0
    points = following[1].shape[0] // (9 * obs) if following else 0
    out = pl.pallas_call(
        functools.partial(update_kernel, obs, points),
        out_shape=(jax.ShapeDtypeStruct(state.shape, F32),) + (rows,) * more,
        in_specs=[smem] * (1 + more) + [vmem] * 3 + [hbm],
        out_specs=(hbm,) + (vmem,) * more,
        scratch_shapes=[
            pltpu.VMEM((strips, members, pitch_of(side), cells), F32),
            pltpu.VMEM((3, 2 * LANES, 2 * LANES), BF16),
            pltpu.VMEM((members, 3 * LANES), F32),
            pltpu.VMEM((8, 3 * LANES), F32),
            pltpu.VMEM((side * members, LANES), F32),
            pltpu.SemaphoreType.DMA((strips,)),
            pltpu.SemaphoreType.DMA((strips,)),
        ]
        + [pltpu.VMEM((3, members, LANES), F32)] * bool(following),
        compiler_params=pltpu.CompilerParams(vmem_limit_bytes=VMEM_LIMIT),
    )(pos, *following, *chunks, state)
    return out


def per_device(prior_state, stencil, weights, obs_values, obs_errors, radius):
    members, side, _, cells = prior_state.shape
    batches, _, _, obs, points = stencil.shape
    lon_index = lax.axis_index("lon")
    lat_index = lax.axis_index("lat")
    lat_total = side * lax.axis_size("lat")
    state = prior_state.reshape(members, side * side, cells)

    own_meta = jnp.concatenate(
        [stencil.reshape(batches, obs * points).astype(F32) + 1.0, weights.reshape(batches, obs * points)]
    )
    first = stencil[:, 0, 0, :, 0]
    about = jnp.stack(
        [
            obs_values[:, 0, 0],
            obs_errors[:, 0, 0],
            (first // (lat_total * cells)).astype(F32),
            (first // cells % lat_total).astype(F32),
            (radius[:, 0, 0] + 1).astype(F32),
        ],
        axis=1,
    )
    about = jnp.pad(about, ((0, 0), (0, 3), (0, LANES - obs)))
    before, after = neighbours(own_meta, "lat")
    row_meta = jnp.concatenate([before, own_meta, after, about.reshape(batches * 8, LANES)])
    before, after = neighbours(row_meta, "lon")
    lon_meta = jnp.stack([before, row_meta, after])
    abouts = lon_meta[:, 3 * 2 * batches :].reshape(3, batches, 8, LANES)
    meta = lon_meta[:, : 3 * 2 * batches].reshape(9, 2, batches, obs * points)
    rows = meta[:, 0].astype(jnp.int32) - 1
    block_lon = rows // (lat_total * cells) - lon_index * side
    block_lat = rows // cells % lat_total - lat_index * side
    here = (rows >= 0) & (block_lon >= 0) & (block_lon < side) & (block_lat >= 0) & (block_lat < side)
    loc = jnp.where(here, (block_lon * side + block_lat) * cells + rows % cells, -1)
    code = jnp.max(here.astype(jnp.int32).reshape(9, batches, obs // WORD, WORD, points), axis=-1)
    code = jnp.sum(code * (1 << jnp.arange(WORD, dtype=jnp.int32)), axis=-1)
    loc = jnp.moveaxis(loc, 1, 0).reshape(batches, -1)
    code = jnp.moveaxis(code, 1, 0).reshape(batches, -1)
    w = jnp.moveaxis(meta[:, 1], 1, 0).reshape(batches, -1)

    pos = jnp.stack([lon_index, lat_index]).astype(jnp.int32)

    means = []
    sums = first_pick(code[0], loc[0], w[0], state, side, obs, points)
    for batch in range(batches):
        to_before, to_own, to_after = sums
        size = lax.axis_size("lat")
        from_before = lax.ppermute(to_after, "lat", [(i, i + 1) for i in range(size - 1)])
        from_after = lax.ppermute(to_before, "lat", [(i + 1, i) for i in range(size - 1)])
        summed = from_before + to_own + from_after
        before, after = neighbours(summed, "lon")
        before2, after2 = neighbours(summed, "lon", 2)
        around = (before2, before, summed, after, after2)
        pack, mean = observe(around, tuple(abouts[:, batch]), obs)
        before, after = neighbours(pack, "lat")
        following = (code[batch + 1], loc[batch + 1], w[batch + 1]) if batch + 1 < batches else ()
        state, *sums = update(pos, (before, pack, after), state, side, obs, following)
        means.append(mean[0, obs : 2 * obs])
    return state.reshape(prior_state.shape), jnp.stack(means)[:, None, None, :]


def solution(mesh):
    placed = (
        P(None, "lon", "lat", None),
        P(None, "lon", "lat", None, None),
        P(None, "lon", "lat", None, None),
        P(None, "lon", "lat", None),
        P(None, "lon", "lat", None),
        P(None, "lon", "lat", None),
    )
    return jax.shard_map(
        per_device,
        mesh=mesh,
        in_specs=placed,
        out_specs=(P(None, "lon", "lat", None), P(None, "lon", "lat", None)),
        check_vma=False,
    )
```

```python
import functools
import jax
import jax.numpy as jnp
from jax import lax
from jax.experimental import pallas as pl
from jax.experimental.pallas import tpu as pltpu
from jax.sharding import PartitionSpec as P

EPS = 1e-06
LANES = 128
WORD = 8
F32 = jnp.float32
BF16 = jnp.bfloat16
VMEM_LIMIT = 48 * 1024 * 1024
UNROLL = 4
GROUP = 16


def pitch_of(side):
    return side + 8 if side % 16 == 0 else side


def neighbours(array, axis, distance=1):
    size = lax.axis_size(axis)
    up = [(i, i + distance) for i in range(size - distance)]
    down = [(j, i) for i, j in up]
    return lax.ppermute(array, axis, up), lax.ppermute(array, axis, down)


def split(x):
    high = x.astype(BF16)
    return high, (x - high.astype(F32)).astype(BF16)


def thirds(x):
    high = x.astype(BF16)
    rest = x - high.astype(F32)
    middle = rest.astype(BF16)
    return high, middle, (rest - middle.astype(F32)).astype(BF16)


def pick(obs, points, side, pitch, members, code_ref, loc_ref, w_ref, held, sums):
    lane = lax.broadcasted_iota(jnp.int32, (members, LANES), 1)
    sums[...] = jnp.zeros_like(sums)

    def one(group, o):
        acc = jnp.zeros((members, LANES), F32)
        for s in range(points):
            at = (group * obs + o) * points + s
            loc = loc_ref[at]
            w = jnp.where(loc >= 0, w_ref[at], 0.0)
            loc = jnp.maximum(loc, 0)
            block = loc // LANES
            start = (block // side) * (members * pitch) + block % side
            x = held[pl.ds(start, members, stride=pitch), :]
            acc = acc + jnp.where(lane == loc % LANES, x * w, 0.0)
        total = jnp.sum(acc, axis=1, keepdims=True)
        return jnp.where(lane == (group // 3) * obs + o, total, 0.0)

    @pl.loop(0, obs // UNROLL)
    def _(t):
        found = [one(4, t * UNROLL + u) for u in range(UNROLL)]
        sums[1] = sums[1] + sum(found[1:], found[0])

    per_group = obs // WORD

    @pl.loop(0, 9 * per_group)
    def _(t):
        word = code_ref[t]

        @pl.when((word > 0) & (t // per_group != 4))
        def _():
            @pl.loop(0, WORD)
            def _(k):
                @pl.when((word // (1 << k)) % 2 == 1)
                def _():
                    group = t // per_group
                    sums[group % 3] = sums[group % 3] + one(group, (t % per_group) * WORD + k)


def strips_in(state_ref, st_ref, side, sem):
    return lambda p: pltpu.make_async_copy(
        state_ref.at[:, pl.ds(p * side, side), :], st_ref.at[p, :, pl.ds(0, side), :], sem.at[p]
    )


def pick_kernel(obs, points, code_ref, loc_ref, w_ref, state_ref, before_ref, own_ref, after_ref, st_ref, sums, sem):
    strips, members, pitch, cells = st_ref.shape
    side = state_ref.shape[1] // strips
    copy = strips_in(state_ref, st_ref, side, sem)
    for p in range(strips):
        copy(p).start()
    for p in range(strips):
        copy(p).wait()
    held = st_ref.reshape(strips * members * pitch, cells)
    pick(obs, points, side, pitch, members, code_ref, loc_ref, w_ref, held, sums)
    for j, out in enumerate((before_ref, own_ref, after_ref)):
        out[...] = sums[j]


def first_pick(code, loc, w, state, side, obs, points):
    members, blocks, cells = state.shape
    strips = blocks // side
    rows = jax.ShapeDtypeStruct((members, LANES), F32)
    smem = pl.BlockSpec(memory_space=pltpu.SMEM)
    vmem = pl.BlockSpec(memory_space=pltpu.VMEM)
    return pl.pallas_call(
        functools.partial(pick_kernel, obs, points),
        out_shape=(rows,) * 3,
        in_specs=[smem, smem, smem, pl.BlockSpec(memory_space=pl.ANY)],
        out_specs=(vmem,) * 3,
        scratch_shapes=[
            pltpu.VMEM((strips, members, pitch_of(side), cells), F32),
            pltpu.VMEM((3, members, LANES), F32),
            pltpu.SemaphoreType.DMA((strips,)),
        ],
        compiler_params=pltpu.CompilerParams(vmem_limit_bytes=VMEM_LIMIT),
    )(code, loc, w, state)


def observe_kernel(obs, lon_ref, rows_ref, *refs):
    abouts, (pack_ref, mean_ref) = refs[:3], refs[3:]
    devices, members, _ = rows_ref.shape
    lane = lax.broadcasted_iota(jnp.int32, (1, LANES), 1)

    def placed(x, source, target):
        shift = (target - source) * obs % LANES
        x = x if shift == 0 else pltpu.roll(x, shift, 1)
        return jnp.where((lane >= target * obs) & (lane < (target + 1) * obs), x, 0.0)

    sums = []
    for k in range(-2, 3):
        at = lon_ref[0] + k
        inside = ((at >= 0) & (at < devices)).astype(F32)
        sums.append(rows_ref[jnp.clip(at, 0, devices - 1)] * inside)
    ensemble, about = 0.0, 0.0
    for t in range(3):
        for source in range(3):
            ensemble = ensemble + placed(sums[t + 2 - source], source, t)
        about = about + placed(abouts[t][...], 0, t)
    values = about[0:1, :]
    known = about[4:5, :] > 0.0
    errors = jnp.where(known, about[1:2, :], 1.0)
    mean = jnp.sum(ensemble, axis=0, keepdims=True) / members
    anomaly = ensemble - mean
    spread = jnp.sum(anomaly * anomaly, axis=0, keepdims=True) / (members - 1) + EPS
    post_var = 1.0 / (1.0 / spread + 1.0 / errors)
    post_mean = post_var * (mean / spread + values / errors)
    delta = (post_mean - mean) + (jnp.sqrt(post_var / spread) - 1.0) * anomaly
    gain = anomaly / ((members - 1) * spread)
    pack_ref[0:members, :] = jnp.where(known, gain, 0.0)
    pack_ref[members : 2 * members, :] = jnp.where(known, delta, 0.0)
    pack_ref[2 * members :, :] = about
    mean_ref[...] = jnp.broadcast_to(mean, mean_ref.shape)


def observe(lon, sums, abouts, obs):
    members = sums.shape[1]
    vmem = pl.BlockSpec(memory_space=pltpu.VMEM)
    return pl.pallas_call(
        functools.partial(observe_kernel, obs),
        out_shape=(
            jax.ShapeDtypeStruct((2 * members + 8, LANES), F32),
            jax.ShapeDtypeStruct((8, LANES), F32),
        ),
        in_specs=[pl.BlockSpec(memory_space=pltpu.SMEM)] + [vmem] * 4,
        out_specs=(vmem, vmem),
    )(lon, sums, *abouts)


def order(about, lon_first, lat_first, side):
    lon, lat, reach = about[2:3, :], about[3:4, :], about[4:5, :]
    lon_gap = jnp.maximum(jnp.maximum(lon_first - lon, lon - (lon_first + side - 1)), 0.0)
    lat_gap = jnp.maximum(jnp.maximum(lat_first - lat, lat - (lat_first + side - 1)), 0.0)
    reached = reach > jnp.maximum(lon_gap, lat_gap)
    cover = jnp.where(lon < lon_first, reach - lon_gap, 2.0 * LANES)
    return jnp.where(reached, cover, -1.0)


def update_kernel(obs, points, *refs):
    if points:
        pos_ref, code_ref, loc_ref, ow_ref, c0_ref, c1_ref, c2_ref, state_ref = refs[:8]
        out_ref, before_ref, own_ref, after_ref, sums = refs[8:12] + refs[-1:]
        st_ref, w_ref, delta_ref, about_ref, a_ref, in_sem, out_sem = refs[12:-1]
    else:
        pos_ref, c0_ref, c1_ref, c2_ref, state_ref, out_ref = refs[:6]
        st_ref, w_ref, delta_ref, about_ref, a_ref, in_sem, out_sem = refs[6:]
    strips, members, pitch, cells = st_ref.shape
    side = state_ref.shape[1] // strips
    rows = members * pitch
    copy_in = strips_in(state_ref, st_ref, side, in_sem)

    def copy_out(p):
        return pltpu.make_async_copy(
            st_ref.at[p, :, pl.ds(0, side), :], out_ref.at[:, pl.ds(p * side, side), :], out_sem.at[p]
        )

    for p in range(strips):
        copy_in(p).start()

    lon_first = (pos_ref[0] * side).astype(F32)
    lat_first = (pos_ref[1] * side).astype(F32)
    near = [
        (c[0:members, :], c[members : 2 * members, :], c[2 * members : 2 * members + 8, :])
        for c in (c0_ref, c1_ref, c2_ref)
    ]
    keys = [order(about, lon_first, lat_first, side) for _, _, about in near]
    lane = lax.broadcasted_iota(jnp.int32, (LANES, LANES), 1)
    sub = lax.broadcasted_iota(jnp.int32, (LANES, LANES), 0)
    picks = []
    for i in range(3):
        mine = jnp.broadcast_to(keys[i], (LANES, LANES)).T
        ahead = jnp.zeros((LANES, LANES), F32)
        for j in range(3):
            before = keys[j] > mine
            if j < i:
                before = before | (keys[j] == mine)
            elif j == i:
                before = before | ((keys[j] == mine) & (lane < sub))
            ahead = ahead + jnp.where(before, 1.0, 0.0)
        rank = jnp.sum(ahead, axis=1, keepdims=True)
        wide = lax.broadcasted_iota(jnp.int32, (LANES, 3 * LANES), 1).astype(F32)
        picks.append(jnp.where(wide == rank, 1.0, 0.0).astype(BF16))
    picks = jnp.concatenate(picks, axis=0)
    gain, delta, about = (jnp.concatenate([n[k] for n in near], axis=1) for k in range(3))
    stack = jnp.concatenate([*thirds(gain), *thirds(delta), about.astype(BF16), jnp.zeros_like(about).astype(BF16)], axis=0)
    moved = jnp.dot(stack, picks, preferred_element_type=F32)
    gain = moved[0:members] + moved[members : 2 * members] + moved[2 * members : 3 * members]
    delta_ref[...] = moved[3 * members : 4 * members] + moved[4 * members : 5 * members] + moved[5 * members : 6 * members]
    about_ref[...] = moved[6 * members : 6 * members + 8]
    for j in range(3):
        part = jnp.concatenate([gain[:, j * LANES : (j + 1) * LANES], jnp.zeros((LANES - members, LANES), F32)], axis=0)
        high, low = split(part.T)
        both = jnp.concatenate([high, low], axis=1)
        w_ref[j, 0:LANES, :] = both
        w_ref[j, LANES:, :] = both

    held = st_ref.reshape(strips * rows, cells)
    lat = lat_first + lax.broadcasted_iota(jnp.int32, (side, 1), 0).astype(F32)

    @pl.loop(0, strips)
    def _(p):
        lon_here = lon_first + p.astype(F32)
        tapers = []
        for j in range(3):
            facts = about_ref[:, j * LANES : (j + 1) * LANES]
            reach = facts[4:5, :]
            gap = jnp.maximum(jnp.abs(lon_here - facts[2:3, :]), jnp.abs(lat - facts[3:4, :]))
            tapers.append(jnp.maximum(0.0, reach - gap) / jnp.maximum(reach, 1.0))

        def matrices(j, first, count):
            delta = delta_ref[:, j * LANES : (j + 1) * LANES]
            left = [jnp.concatenate(split(delta * tapers[j][q : q + 1, :]), axis=1) for q in range(first, first + count)]
            both = jnp.dot(jnp.concatenate(left, axis=0), w_ref[j], preferred_element_type=F32)
            return both[:, :LANES] + both[:, LANES:]

        def finish(more):
            for first in range(0, side, GROUP):
                part = pl.ds(first * members, GROUP * members)
                a = matrices(0, first, GROUP)
                high, low = split(a + a_ref[part, :] if more else a)
                left = jnp.concatenate([high[:, :members], high[:, :members], low[:, :members]], axis=1)
                for q in range(0, GROUP, 2):
                    at = [pl.ds(p * rows + first + q + k, members, stride=pitch) for k in range(2)]
                    x = jnp.concatenate([held[at[0], :], held[at[1], :]], axis=1)
                    x_high, x_low = split(x - jnp.sum(x, axis=0, keepdims=True) / members)
                    right = jnp.concatenate([x_high, x_low, x_high], axis=0)
                    change = jnp.dot(left[q * members : (q + 2) * members], right, preferred_element_type=F32)
                    held[at[0], :] = x[:, :cells] + change[:members, :cells]
                    held[at[1], :] = x[:, cells:] + change[members:, cells:]

        far = jnp.max(jnp.maximum(tapers[1], tapers[2])) > 0.0
        copy_in(p).wait()

        @pl.when(far)
        def _():
            for first in range(0, side, GROUP):
                a_ref[pl.ds(first * members, GROUP * members), :] = matrices(1, first, GROUP)

            @pl.when(jnp.max(tapers[2]) > 0.0)
            def _():
                for first in range(0, side, GROUP):
                    a_ref[pl.ds(first * members, GROUP * members), :] += matrices(2, first, GROUP)

            finish(True)

        @pl.when(jnp.logical_not(far))
        def _():
            finish(False)

        copy_out(p).start()

    if points:
        pick(obs, points, side, pitch, members, code_ref, loc_ref, ow_ref, held, sums)
        for j, out in enumerate((before_ref, own_ref, after_ref)):
            out[...] = sums[j]
    for p in range(strips):
        copy_out(p).wait()


def update(pos, chunks, state, side, obs, following=()):
    members, blocks, cells = state.shape
    strips = blocks // side
    smem = pl.BlockSpec(memory_space=pltpu.SMEM)
    vmem = pl.BlockSpec(memory_space=pltpu.VMEM)
    hbm = pl.BlockSpec(memory_space=pl.ANY)
    rows = jax.ShapeDtypeStruct((members, LANES), F32)
    more = 3 if following else 0
    points = following[1].shape[0] // (9 * obs) if following else 0
    out = pl.pallas_call(
        functools.partial(update_kernel, obs, points),
        out_shape=(jax.ShapeDtypeStruct(state.shape, F32),) + (rows,) * more,
        in_specs=[smem] * (1 + more) + [vmem] * 3 + [hbm],
        out_specs=(hbm,) + (vmem,) * more,
        scratch_shapes=[
            pltpu.VMEM((strips, members, pitch_of(side), cells), F32),
            pltpu.VMEM((3, 2 * LANES, 2 * LANES), BF16),
            pltpu.VMEM((members, 3 * LANES), F32),
            pltpu.VMEM((8, 3 * LANES), F32),
            pltpu.VMEM((side * members, LANES), F32),
            pltpu.SemaphoreType.DMA((strips,)),
            pltpu.SemaphoreType.DMA((strips,)),
        ]
        + [pltpu.VMEM((3, members, LANES), F32)] * bool(following),
        compiler_params=pltpu.CompilerParams(vmem_limit_bytes=VMEM_LIMIT),
    )(pos, *following, *chunks, state)
    return out


def per_device(prior_state, stencil, weights, obs_values, obs_errors, radius):
    members, side, _, cells = prior_state.shape
    batches, _, _, obs, points = stencil.shape
    lon_index = lax.axis_index("lon")
    lat_index = lax.axis_index("lat")
    lat_total = side * lax.axis_size("lat")
    state = prior_state.reshape(members, side * side, cells)

    own_meta = jnp.concatenate(
        [stencil.reshape(batches, obs * points).astype(F32) + 1.0, weights.reshape(batches, obs * points)]
    )
    first = stencil[:, 0, 0, :, 0]
    about = jnp.stack(
        [
            obs_values[:, 0, 0],
            obs_errors[:, 0, 0],
            (first // (lat_total * cells)).astype(F32),
            (first // cells % lat_total).astype(F32),
            (radius[:, 0, 0] + 1).astype(F32),
        ],
        axis=1,
    )
    about = jnp.pad(about, ((0, 0), (0, 3), (0, LANES - obs)))
    before, after = neighbours(own_meta, "lat")
    row_meta = jnp.concatenate([before, own_meta, after, about.reshape(batches * 8, LANES)])
    before, after = neighbours(row_meta, "lon")
    lon_meta = jnp.stack([before, row_meta, after])
    abouts = lon_meta[:, 3 * 2 * batches :].reshape(3, batches, 8, LANES)
    meta = lon_meta[:, : 3 * 2 * batches].reshape(9, 2, batches, obs * points)
    rows = meta[:, 0].astype(jnp.int32) - 1
    block_lon = rows // (lat_total * cells) - lon_index * side
    block_lat = rows // cells % lat_total - lat_index * side
    here = (rows >= 0) & (block_lon >= 0) & (block_lon < side) & (block_lat >= 0) & (block_lat < side)
    loc = jnp.where(here, (block_lon * side + block_lat) * cells + rows % cells, -1)
    code = jnp.max(here.astype(jnp.int32).reshape(9, batches, obs // WORD, WORD, points), axis=-1)
    code = jnp.sum(code * (1 << jnp.arange(WORD, dtype=jnp.int32)), axis=-1)
    loc = jnp.moveaxis(loc, 1, 0).reshape(batches, -1)
    code = jnp.moveaxis(code, 1, 0).reshape(batches, -1)
    w = jnp.moveaxis(meta[:, 1], 1, 0).reshape(batches, -1)

    pos = jnp.stack([lon_index, lat_index]).astype(jnp.int32)

    means = []
    sums = first_pick(code[0], loc[0], w[0], state, side, obs, points)
    for batch in range(batches):
        to_before, to_own, to_after = sums
        size = lax.axis_size("lat")
        from_before = lax.ppermute(to_after, "lat", [(i, i + 1) for i in range(size - 1)])
        from_after = lax.ppermute(to_before, "lat", [(i + 1, i) for i in range(size - 1)])
        summed = from_before + to_own + from_after
        everywhere = jnp.broadcast_to(summed, (lax.axis_size("lon"),) + summed.shape)
        row_sums = lax.all_to_all(everywhere, "lon", 0, 0, tiled=True)
        pack, mean = observe(pos, row_sums, tuple(abouts[:, batch]), obs)
        before, after = neighbours(pack, "lat")
        following = (code[batch + 1], loc[batch + 1], w[batch + 1]) if batch + 1 < batches else ()
        state, *sums = update(pos, (before, pack, after), state, side, obs, following)
        means.append(mean[0, obs : 2 * obs])
    return state.reshape(prior_state.shape), jnp.stack(means)[:, None, None, :]


def solution(mesh):
    placed = (
        P(None, "lon", "lat", None),
        P(None, "lon", "lat", None, None),
        P(None, "lon", "lat", None, None),
        P(None, "lon", "lat", None),
        P(None, "lon", "lat", None),
        P(None, "lon", "lat", None),
    )
    return jax.shard_map(
        per_device,
        mesh=mesh,
        in_specs=placed,
        out_specs=(P(None, "lon", "lat", None), P(None, "lon", "lat", None)),
        check_vma=False,
    )
```

```python
import functools
import jax
import jax.numpy as jnp
from jax import lax
from jax.experimental import pallas as pl
from jax.experimental.pallas import tpu as pltpu
from jax.sharding import PartitionSpec as P

EPS = 1e-06
LANES = 128
WORD = 8
F32 = jnp.float32
BF16 = jnp.bfloat16
VMEM_LIMIT = 48 * 1024 * 1024
UNROLL = 4
GROUP = 16
PARTS = 4


def pitch_of(side):
    return side + 8 if side % 16 == 0 else side


def neighbours(array, axis, distance=1):
    size = lax.axis_size(axis)
    up = [(i, i + distance) for i in range(size - distance)]
    down = [(j, i) for i, j in up]
    return lax.ppermute(array, axis, up), lax.ppermute(array, axis, down)


def split(x):
    high = x.astype(BF16)
    return high, (x - high.astype(F32)).astype(BF16)


def thirds(x):
    high = x.astype(BF16)
    rest = x - high.astype(F32)
    middle = rest.astype(BF16)
    return high, middle, (rest - middle.astype(F32)).astype(BF16)


def pick(obs, points, side, pitch, members, code_ref, loc_ref, w_ref, held, sums):
    lane = lax.broadcasted_iota(jnp.int32, (members, LANES), 1)
    sums[...] = jnp.zeros_like(sums)

    def one(group, o):
        acc = jnp.zeros((members, LANES), F32)
        for s in range(points):
            at = (group * obs + o) * points + s
            loc = loc_ref[at]
            w = jnp.where(loc >= 0, w_ref[at], 0.0)
            loc = jnp.maximum(loc, 0)
            block = loc // LANES
            start = (block // side) * (members * pitch) + block % side
            x = held[pl.ds(start, members, stride=pitch), :]
            acc = acc + jnp.where(lane == loc % LANES, x * w, 0.0)
        total = jnp.sum(acc, axis=1, keepdims=True)
        return jnp.where(lane == (group // 3) * obs + o, total, 0.0)

    @pl.loop(0, obs // UNROLL)
    def _(t):
        found = [one(4, t * UNROLL + u) for u in range(UNROLL)]
        sums[1] = sums[1] + sum(found[1:], found[0])

    per_group = obs // WORD

    @pl.loop(0, 9 * per_group)
    def _(t):
        word = code_ref[t]

        group = t // per_group

        @pl.when((word > 0) & (group != 4))
        def _():
            def step(left):
                low = left & -left
                bit = sum(((low >> k) > 0).astype(jnp.int32) for k in range(1, WORD))
                sums[group % 3] = sums[group % 3] + one(group, (t % per_group) * WORD + bit)
                return left - low

            lax.while_loop(lambda left: left > 0, step, word)


def strips_in(state_ref, st_ref, side, sem):
    return lambda p: pltpu.make_async_copy(
        state_ref.at[:, pl.ds(p * side, side), :], st_ref.at[p, :, pl.ds(0, side), :], sem.at[p]
    )


def pick_kernel(obs, points, code_ref, loc_ref, w_ref, state_ref, before_ref, own_ref, after_ref, st_ref, sums, sem):
    strips, members, pitch, cells = st_ref.shape
    side = state_ref.shape[1] // strips
    copy = strips_in(state_ref, st_ref, side, sem)
    for p in range(strips):
        copy(p).start()
    for p in range(strips):
        copy(p).wait()
    held = st_ref.reshape(strips * members * pitch, cells)
    pick(obs, points, side, pitch, members, code_ref, loc_ref, w_ref, held, sums)
    for j, out in enumerate((before_ref, own_ref, after_ref)):
        out[...] = sums[j]


def first_pick(code, loc, w, state, side, obs, points):
    members, blocks, cells = state.shape
    strips = blocks // side
    rows = jax.ShapeDtypeStruct((members, LANES), F32)
    smem = pl.BlockSpec(memory_space=pltpu.SMEM)
    vmem = pl.BlockSpec(memory_space=pltpu.VMEM)
    return pl.pallas_call(
        functools.partial(pick_kernel, obs, points),
        out_shape=(rows,) * 3,
        in_specs=[smem, smem, smem, pl.BlockSpec(memory_space=pl.ANY)],
        out_specs=(vmem,) * 3,
        scratch_shapes=[
            pltpu.VMEM((strips, members, pitch_of(side), cells), F32),
            pltpu.VMEM((3, members, LANES), F32),
            pltpu.SemaphoreType.DMA((strips,)),
        ],
        compiler_params=pltpu.CompilerParams(vmem_limit_bytes=VMEM_LIMIT),
    )(code, loc, w, state)


def observe_kernel(obs, lon_ref, rows_ref, *refs):
    abouts, (pack_ref, mean_ref) = refs[:3], refs[3:]
    devices, members, _ = rows_ref.shape
    lane = lax.broadcasted_iota(jnp.int32, (1, LANES), 1)

    def placed(x, source, target):
        shift = (target - source) * obs % LANES
        x = x if shift == 0 else pltpu.roll(x, shift, 1)
        return jnp.where((lane >= target * obs) & (lane < (target + 1) * obs), x, 0.0)

    sums = []
    for k in range(-2, 3):
        at = lon_ref[0] + k
        inside = ((at >= 0) & (at < devices)).astype(F32)
        sums.append(rows_ref[jnp.clip(at, 0, devices - 1)] * inside)
    ensemble, about = 0.0, 0.0
    for t in range(3):
        for source in range(3):
            ensemble = ensemble + placed(sums[t + 2 - source], source, t)
        about = about + placed(abouts[t][...], 0, t)
    values = about[0:1, :]
    known = about[4:5, :] > 0.0
    errors = jnp.where(known, about[1:2, :], 1.0)
    mean = jnp.sum(ensemble, axis=0, keepdims=True) / members
    anomaly = ensemble - mean
    spread = jnp.sum(anomaly * anomaly, axis=0, keepdims=True) / (members - 1) + EPS
    post_var = 1.0 / (1.0 / spread + 1.0 / errors)
    post_mean = post_var * (mean / spread + values / errors)
    delta = (post_mean - mean) + (jnp.sqrt(post_var / spread) - 1.0) * anomaly
    gain = anomaly / ((members - 1) * spread)
    pack_ref[0:members, :] = jnp.where(known, gain, 0.0)
    pack_ref[members : 2 * members, :] = jnp.where(known, delta, 0.0)
    pack_ref[2 * members :, :] = about
    mean_ref[...] = jnp.broadcast_to(mean, mean_ref.shape)


def observe(lon, sums, abouts, obs):
    members = sums.shape[1]
    vmem = pl.BlockSpec(memory_space=pltpu.VMEM)
    return pl.pallas_call(
        functools.partial(observe_kernel, obs),
        out_shape=(
            jax.ShapeDtypeStruct((2 * members + 8, LANES), F32),
            jax.ShapeDtypeStruct((8, LANES), F32),
        ),
        in_specs=[pl.BlockSpec(memory_space=pltpu.SMEM)] + [vmem] * 4,
        out_specs=(vmem, vmem),
    )(lon, sums, *abouts)


def reached(about, lon_first, lon_last, lat_first, lat_last):
    lon, lat, reach = about[2:3, :], about[3:4, :], about[4:5, :]
    lon_gap = jnp.maximum(jnp.maximum(lon_first - lon, lon - lon_last), 0.0)
    lat_gap = jnp.maximum(jnp.maximum(lat_first - lat, lat - lat_last), 0.0)
    return jnp.where(reach > jnp.maximum(lon_gap, lat_gap), 1.0, 0.0)


def update_kernel(obs, points, *refs):
    if points:
        pos_ref, code_ref, loc_ref, ow_ref, c0_ref, c1_ref, c2_ref, state_ref = refs[:8]
        out_ref, before_ref, own_ref, after_ref, sums = refs[8:12] + refs[-1:]
        st_ref, w_ref, delta_ref, about_ref, a_ref, in_sem, out_sem = refs[12:-1]
    else:
        pos_ref, c0_ref, c1_ref, c2_ref, state_ref, out_ref = refs[:6]
        st_ref, w_ref, delta_ref, about_ref, a_ref, in_sem, out_sem = refs[6:]
    strips, members, pitch, cells = st_ref.shape
    side = state_ref.shape[1] // strips
    rows = members * pitch
    copy_in = strips_in(state_ref, st_ref, side, in_sem)

    def copy_out(p):
        return pltpu.make_async_copy(
            st_ref.at[p, :, pl.ds(0, side), :], out_ref.at[:, pl.ds(p * side, side), :], out_sem.at[p]
        )

    for p in range(strips):
        copy_in(p).start()

    lon_first = (pos_ref[0] * side).astype(F32)
    lat_first = (pos_ref[1] * side).astype(F32)
    near = [
        (c[0:members, :], c[members : 2 * members, :], c[2 * members : 2 * members + 8, :])
        for c in (c0_ref, c1_ref, c2_ref)
    ]
    gain, delta, about = (jnp.concatenate([n[k] for n in near], axis=1) for k in range(3))
    stack = jnp.concatenate([*thirds(gain), *thirds(delta), about.astype(BF16), jnp.zeros_like(about).astype(BF16)], axis=0)
    lane = lax.broadcasted_iota(jnp.int32, (3 * LANES, 3 * LANES), 1)
    sub = lax.broadcasted_iota(jnp.int32, (3 * LANES, 3 * LANES), 0)
    earlier = jnp.where(sub < lane, 1.0, 0.0).astype(BF16)
    wide = lax.broadcasted_iota(jnp.int32, (LANES, 3 * LANES), 1).astype(F32)
    span = strips // PARTS
    keys = [
        jnp.concatenate(
            [
                reached(n[2], lon_first + h * span, lon_first + (h + 1) * span - 1, lat_first, lat_first + side - 1)
                for n in near
            ],
            axis=1,
        )
        for h in range(PARTS)
    ]
    keys = jnp.concatenate(keys + [jnp.zeros((8 - PARTS, 3 * LANES), F32)], axis=0)
    keys = jnp.concatenate([keys, jnp.zeros_like(keys)], axis=0)
    ahead = jnp.dot(keys.astype(BF16), earlier, preferred_element_type=F32)
    place = lax.broadcasted_iota(jnp.int32, keys.shape, 1).astype(F32)
    ranks = jnp.where(keys > 0.0, ahead, jnp.sum(keys, axis=1, keepdims=True) + place - ahead)
    for h in range(PARTS):
        picks = []
        for i in range(3):
            rank = jnp.broadcast_to(ranks[h : h + 1, i * LANES : (i + 1) * LANES], (LANES, LANES)).T
            picks.append(jnp.where(wide == jnp.concatenate([rank] * 3, axis=1), 1.0, 0.0).astype(BF16))
        moved = jnp.dot(stack, jnp.concatenate(picks, axis=0), preferred_element_type=F32)
        sorted_gain = moved[0:members] + moved[members : 2 * members] + moved[2 * members : 3 * members]
        delta_ref[h] = moved[3 * members : 4 * members] + moved[4 * members : 5 * members] + moved[5 * members : 6 * members]
        about_ref[h] = moved[6 * members : 6 * members + 8]
        for j in range(3):
            part = sorted_gain[:, j * LANES : (j + 1) * LANES]
            part = jnp.concatenate([part, jnp.zeros((LANES - members, LANES), F32)], axis=0)
            both = jnp.concatenate(split(part.T), axis=1)
            w_ref[h * 3 + j, 0:LANES, :] = both
            w_ref[h * 3 + j, LANES:, :] = both

    held = st_ref.reshape(strips * rows, cells)
    lat = lat_first + lax.broadcasted_iota(jnp.int32, (side, 1), 0).astype(F32)

    @pl.loop(0, strips)
    def _(p):
        lon_here = lon_first + p.astype(F32)
        h = p // span
        tapers = []
        for j in range(3):
            facts = about_ref[h, :, j * LANES : (j + 1) * LANES]
            reach = facts[4:5, :]
            gap = jnp.maximum(jnp.abs(lon_here - facts[2:3, :]), jnp.abs(lat - facts[3:4, :]))
            tapers.append(jnp.maximum(0.0, reach - gap) / jnp.maximum(reach, 1.0))

        def matrices(j, first, count):
            delta = delta_ref[h, :, j * LANES : (j + 1) * LANES]
            left = [jnp.concatenate(split(delta * tapers[j][q : q + 1, :]), axis=1) for q in range(first, first + count)]
            both = jnp.dot(jnp.concatenate(left, axis=0), w_ref[h * 3 + j], preferred_element_type=F32)
            return both[:, :LANES] + both[:, LANES:]

        def finish(more):
            for first in range(0, side, GROUP):
                part = pl.ds(first * members, GROUP * members)
                a = matrices(0, first, GROUP)
                high, low = split(a + a_ref[part, :] if more else a)
                left = jnp.concatenate([high[:, :members], high[:, :members], low[:, :members]], axis=1)
                for q in range(0, GROUP, 2):
                    at = [pl.ds(p * rows + first + q + k, members, stride=pitch) for k in range(2)]
                    x = jnp.concatenate([held[at[0], :], held[at[1], :]], axis=1)
                    x_high, x_low = split(x - jnp.sum(x, axis=0, keepdims=True) / members)
                    right = jnp.concatenate([x_high, x_low, x_high], axis=0)
                    change = jnp.dot(left[q * members : (q + 2) * members], right, preferred_element_type=F32)
                    held[at[0], :] = x[:, :cells] + change[:members, :cells]
                    held[at[1], :] = x[:, cells:] + change[members:, cells:]

        far = jnp.max(jnp.maximum(tapers[1], tapers[2])) > 0.0
        copy_in(p).wait()

        @pl.when(far)
        def _():
            for first in range(0, side, GROUP):
                a_ref[pl.ds(first * members, GROUP * members), :] = matrices(1, first, GROUP)

            @pl.when(jnp.max(tapers[2]) > 0.0)
            def _():
                for first in range(0, side, GROUP):
                    a_ref[pl.ds(first * members, GROUP * members), :] += matrices(2, first, GROUP)

            finish(True)

        @pl.when(jnp.logical_not(far))
        def _():
            finish(False)

        copy_out(p).start()

    if points:
        pick(obs, points, side, pitch, members, code_ref, loc_ref, ow_ref, held, sums)
        for j, out in enumerate((before_ref, own_ref, after_ref)):
            out[...] = sums[j]
    for p in range(strips):
        copy_out(p).wait()


def update(pos, chunks, state, side, obs, following=()):
    members, blocks, cells = state.shape
    strips = blocks // side
    smem = pl.BlockSpec(memory_space=pltpu.SMEM)
    vmem = pl.BlockSpec(memory_space=pltpu.VMEM)
    hbm = pl.BlockSpec(memory_space=pl.ANY)
    rows = jax.ShapeDtypeStruct((members, LANES), F32)
    more = 3 if following else 0
    points = following[1].shape[0] // (9 * obs) if following else 0
    out = pl.pallas_call(
        functools.partial(update_kernel, obs, points),
        out_shape=(jax.ShapeDtypeStruct(state.shape, F32),) + (rows,) * more,
        in_specs=[smem] * (1 + more) + [vmem] * 3 + [hbm],
        out_specs=(hbm,) + (vmem,) * more,
        scratch_shapes=[
            pltpu.VMEM((strips, members, pitch_of(side), cells), F32),
            pltpu.VMEM((3 * PARTS, 2 * LANES, 2 * LANES), BF16),
            pltpu.VMEM((PARTS, members, 3 * LANES), F32),
            pltpu.VMEM((PARTS, 8, 3 * LANES), F32),
            pltpu.VMEM((side * members, LANES), F32),
            pltpu.SemaphoreType.DMA((strips,)),
            pltpu.SemaphoreType.DMA((strips,)),
        ]
        + [pltpu.VMEM((3, members, LANES), F32)] * bool(following),
        compiler_params=pltpu.CompilerParams(vmem_limit_bytes=VMEM_LIMIT),
    )(pos, *following, *chunks, state)
    return out


def per_device(prior_state, stencil, weights, obs_values, obs_errors, radius):
    members, side, _, cells = prior_state.shape
    batches, _, _, obs, points = stencil.shape
    lon_index = lax.axis_index("lon")
    lat_index = lax.axis_index("lat")
    lat_total = side * lax.axis_size("lat")
    state = prior_state.reshape(members, side * side, cells)

    own_meta = jnp.concatenate(
        [stencil.reshape(batches, obs * points).astype(F32) + 1.0, weights.reshape(batches, obs * points)]
    )
    first = stencil[:, 0, 0, :, 0]
    about = jnp.stack(
        [
            obs_values[:, 0, 0],
            obs_errors[:, 0, 0],
            (first // (lat_total * cells)).astype(F32),
            (first // cells % lat_total).astype(F32),
            (radius[:, 0, 0] + 1).astype(F32),
        ],
        axis=1,
    )
    about = jnp.pad(about, ((0, 0), (0, 3), (0, LANES - obs)))
    before, after = neighbours(own_meta, "lat")
    row_meta = jnp.concatenate([before, own_meta, after, about.reshape(batches * 8, LANES)])
    before, after = neighbours(row_meta, "lon")
    lon_meta = jnp.stack([before, row_meta, after])
    abouts = lon_meta[:, 3 * 2 * batches :].reshape(3, batches, 8, LANES)
    meta = lon_meta[:, : 3 * 2 * batches].reshape(9, 2, batches, obs * points)
    rows = meta[:, 0].astype(jnp.int32) - 1
    block_lon = rows // (lat_total * cells) - lon_index * side
    block_lat = rows // cells % lat_total - lat_index * side
    here = (rows >= 0) & (block_lon >= 0) & (block_lon < side) & (block_lat >= 0) & (block_lat < side)
    loc = jnp.where(here, (block_lon * side + block_lat) * cells + rows % cells, -1)
    code = jnp.max(here.astype(jnp.int32).reshape(9, batches, obs // WORD, WORD, points), axis=-1)
    code = jnp.sum(code * (1 << jnp.arange(WORD, dtype=jnp.int32)), axis=-1)
    loc = jnp.moveaxis(loc, 1, 0).reshape(batches, -1)
    code = jnp.moveaxis(code, 1, 0).reshape(batches, -1)
    w = jnp.moveaxis(meta[:, 1], 1, 0).reshape(batches, -1)

    pos = jnp.stack([lon_index, lat_index]).astype(jnp.int32)

    means = []
    sums = first_pick(code[0], loc[0], w[0], state, side, obs, points)
    for batch in range(batches):
        to_before, to_own, to_after = sums
        size = lax.axis_size("lat")
        from_before = lax.ppermute(to_after, "lat", [(i, i + 1) for i in range(size - 1)])
        from_after = lax.ppermute(to_before, "lat", [(i + 1, i) for i in range(size - 1)])
        summed = from_before + to_own + from_after
        everywhere = jnp.broadcast_to(summed, (lax.axis_size("lon"),) + summed.shape)
        row_sums = lax.all_to_all(everywhere, "lon", 0, 0, tiled=True)
        pack, mean = observe(pos, row_sums, tuple(abouts[:, batch]), obs)
        before, after = neighbours(pack, "lat")
        following = (code[batch + 1], loc[batch + 1], w[batch + 1]) if batch + 1 < batches else ()
        state, *sums = update(pos, (before, pack, after), state, side, obs, following)
        means.append(mean[0, obs : 2 * obs])
    return state.reshape(prior_state.shape), jnp.stack(means)[:, None, None, :]


def solution(mesh):
    placed = (
        P(None, "lon", "lat", None),
        P(None, "lon", "lat", None, None),
        P(None, "lon", "lat", None, None),
        P(None, "lon", "lat", None),
        P(None, "lon", "lat", None),
        P(None, "lon", "lat", None),
    )
    return jax.shard_map(
        per_device,
        mesh=mesh,
        in_specs=placed,
        out_specs=(P(None, "lon", "lat", None), P(None, "lon", "lat", None)),
        check_vma=False,
    )
```

```python
import functools
import jax
import jax.numpy as jnp
from jax import lax
from jax.experimental import pallas as pl
from jax.experimental.pallas import tpu as pltpu
from jax.sharding import PartitionSpec as P

EPS = 1e-06
LANES = 128
WORD = 8
F32 = jnp.float32
BF16 = jnp.bfloat16
VMEM_LIMIT = 48 * 1024 * 1024
UNROLL = 4
GROUP = 16
PARTS = 4


def pitch_of(side):
    return side + 8 if side % 16 == 0 else side


def neighbours(array, axis, distance=1):
    size = lax.axis_size(axis)
    up = [(i, i + distance) for i in range(size - distance)]
    down = [(j, i) for i, j in up]
    return lax.ppermute(array, axis, up), lax.ppermute(array, axis, down)


def split(x):
    high = x.astype(BF16)
    return high, (x - high.astype(F32)).astype(BF16)


def thirds(x):
    high = x.astype(BF16)
    rest = x - high.astype(F32)
    middle = rest.astype(BF16)
    return high, middle, (rest - middle.astype(F32)).astype(BF16)


def placed(x, source, target, obs):
    lane = lax.broadcasted_iota(jnp.int32, (1, LANES), 1)
    shift = (target - source) * obs % LANES
    x = x if shift == 0 else pltpu.roll(x, shift, 1)
    return jnp.where((lane >= target * obs) & (lane < (target + 1) * obs), x, 0.0)


def fold_rows(members, obs):
    return -(-members // (LANES // obs * 8)) * 8


def fold(x, slot, obs):
    members = x.shape[0]
    rows = fold_rows(members, obs)
    x = jnp.concatenate([x, jnp.zeros((LANES // obs * rows - members, LANES), F32)], axis=0)
    return sum(placed(x[k * rows : (k + 1) * rows], slot, k, obs) for k in range(LANES // obs))


def pick(obs, points, side, pitch, members, code_ref, loc_ref, w_ref, held, sums):
    lane = lax.broadcasted_iota(jnp.int32, (members, LANES), 1)
    sums[...] = jnp.zeros_like(sums)

    def one(group, o):
        acc = jnp.zeros((members, LANES), F32)
        for s in range(points):
            at = (group * obs + o) * points + s
            loc = loc_ref[at]
            w = jnp.where(loc >= 0, w_ref[at], 0.0)
            loc = jnp.maximum(loc, 0)
            block = loc // LANES
            start = (block // side) * (members * pitch) + block % side
            x = held[pl.ds(start, members, stride=pitch), :]
            acc = acc + jnp.where(lane == loc % LANES, x * w, 0.0)
        total = jnp.sum(acc, axis=1, keepdims=True)
        return jnp.where(lane == (group // 3) * obs + o, total, 0.0)

    @pl.loop(0, obs // UNROLL)
    def _(t):
        found = [one(4, t * UNROLL + u) for u in range(UNROLL)]
        sums[1] = sums[1] + sum(found[1:], found[0])

    per_group = obs // WORD

    @pl.loop(0, 9 * per_group)
    def _(t):
        word = code_ref[t]

        group = t // per_group

        @pl.when((word > 0) & (group != 4))
        def _():
            def step(left):
                low = left & -left
                bit = sum(((low >> k) > 0).astype(jnp.int32) for k in range(1, WORD))
                sums[group % 3] = sums[group % 3] + one(group, (t % per_group) * WORD + bit)
                return left - low

            lax.while_loop(lambda left: left > 0, step, word)


def put_folded(sums, outs, obs):
    for j, out in enumerate(outs):
        for slot in range(3):
            out[slot] = fold(sums[j], slot, obs)


def strips_in(state_ref, st_ref, side, sem):
    return lambda p: pltpu.make_async_copy(
        state_ref.at[:, pl.ds(p * side, side), :], st_ref.at[p, :, pl.ds(0, side), :], sem.at[p]
    )


def pick_kernel(obs, points, code_ref, loc_ref, w_ref, state_ref, before_ref, own_ref, after_ref, st_ref, sums, sem):
    strips, members, pitch, cells = st_ref.shape
    side = state_ref.shape[1] // strips
    copy = strips_in(state_ref, st_ref, side, sem)
    for p in range(strips):
        copy(p).start()
    for p in range(strips):
        copy(p).wait()
    held = st_ref.reshape(strips * members * pitch, cells)
    pick(obs, points, side, pitch, members, code_ref, loc_ref, w_ref, held, sums)
    put_folded(sums, (before_ref, own_ref, after_ref), obs)


def first_pick(code, loc, w, state, side, obs, points):
    members, blocks, cells = state.shape
    strips = blocks // side
    rows = jax.ShapeDtypeStruct((3, fold_rows(members, obs), LANES), F32)
    smem = pl.BlockSpec(memory_space=pltpu.SMEM)
    vmem = pl.BlockSpec(memory_space=pltpu.VMEM)
    return pl.pallas_call(
        functools.partial(pick_kernel, obs, points),
        out_shape=(rows,) * 3,
        in_specs=[smem, smem, smem, pl.BlockSpec(memory_space=pl.ANY)],
        out_specs=(vmem,) * 3,
        scratch_shapes=[
            pltpu.VMEM((strips, members, pitch_of(side), cells), F32),
            pltpu.VMEM((3, members, LANES), F32),
            pltpu.SemaphoreType.DMA((strips,)),
        ],
        compiler_params=pltpu.CompilerParams(vmem_limit_bytes=VMEM_LIMIT),
    )(code, loc, w, state)


def observe_kernel(obs, members, lon_ref, summed_ref, rows_ref, *refs):
    abouts, (pack_ref, mean_ref) = refs[:3], refs[3:]
    devices = rows_ref.shape[0]

    def sums(distance, slot):
        if distance == 0:
            return summed_ref[slot]
        at = lon_ref[0] + distance
        part = rows_ref[jnp.clip(at, 0, devices - 1), slot - 1 if distance < 0 else slot]
        return jnp.where((at >= 0) & (at < devices), part, 0.0)

    pieces = [0.0] * (LANES // obs)
    about = 0.0
    for t in range(3):
        for slot in range(3):
            part = sums(t - slot, slot)
            pieces = [piece + placed(part, k, t, obs) for k, piece in enumerate(pieces)]
        about = about + placed(abouts[t][...], 0, t, obs)
    ensemble = jnp.concatenate(pieces, axis=0)[:members]
    values = about[0:1, :]
    known = about[4:5, :] > 0.0
    errors = jnp.where(known, about[1:2, :], 1.0)
    mean = jnp.sum(ensemble, axis=0, keepdims=True) / members
    anomaly = ensemble - mean
    spread = jnp.sum(anomaly * anomaly, axis=0, keepdims=True) / (members - 1) + EPS
    post_var = 1.0 / (1.0 / spread + 1.0 / errors)
    post_mean = post_var * (mean / spread + values / errors)
    delta = (post_mean - mean) + (jnp.sqrt(post_var / spread) - 1.0) * anomaly
    gain = anomaly / ((members - 1) * spread)
    pack_ref[0:members, :] = jnp.where(known, gain, 0.0)
    pack_ref[members : 2 * members, :] = jnp.where(known, delta, 0.0)
    pack_ref[2 * members :, :] = about
    mean_ref[...] = jnp.broadcast_to(mean, mean_ref.shape)


def observe(lon, summed, rows, abouts, obs, members):
    vmem = pl.BlockSpec(memory_space=pltpu.VMEM)
    return pl.pallas_call(
        functools.partial(observe_kernel, obs, members),
        out_shape=(
            jax.ShapeDtypeStruct((2 * members + 8, LANES), F32),
            jax.ShapeDtypeStruct((8, LANES), F32),
        ),
        in_specs=[pl.BlockSpec(memory_space=pltpu.SMEM)] + [vmem] * 5,
        out_specs=(vmem, vmem),
    )(lon, summed, rows, *abouts)


def reached(about, lon_first, lon_last, lat_first, lat_last):
    lon, lat, reach = about[2:3, :], about[3:4, :], about[4:5, :]
    lon_gap = jnp.maximum(jnp.maximum(lon_first - lon, lon - lon_last), 0.0)
    lat_gap = jnp.maximum(jnp.maximum(lat_first - lat, lat - lat_last), 0.0)
    return jnp.where(reach > jnp.maximum(lon_gap, lat_gap), 1.0, 0.0)


def update_kernel(obs, points, *refs):
    if points:
        pos_ref, code_ref, loc_ref, ow_ref, c0_ref, c1_ref, c2_ref, state_ref = refs[:8]
        out_ref, before_ref, own_ref, after_ref, sums = refs[8:12] + refs[-1:]
        st_ref, w_ref, delta_ref, about_ref, a_ref, in_sem, out_sem = refs[12:-1]
    else:
        pos_ref, c0_ref, c1_ref, c2_ref, state_ref, out_ref = refs[:6]
        st_ref, w_ref, delta_ref, about_ref, a_ref, in_sem, out_sem = refs[6:]
    strips, members, pitch, cells = st_ref.shape
    side = state_ref.shape[1] // strips
    rows = members * pitch
    copy_in = strips_in(state_ref, st_ref, side, in_sem)

    def copy_out(p):
        return pltpu.make_async_copy(
            st_ref.at[p, :, pl.ds(0, side), :], out_ref.at[:, pl.ds(p * side, side), :], out_sem.at[p]
        )

    for p in range(strips):
        copy_in(p).start()

    lon_first = (pos_ref[0] * side).astype(F32)
    lat_first = (pos_ref[1] * side).astype(F32)
    near = [
        (c[0:members, :], c[members : 2 * members, :], c[2 * members : 2 * members + 8, :])
        for c in (c0_ref, c1_ref, c2_ref)
    ]
    gain, delta, about = (jnp.concatenate([n[k] for n in near], axis=1) for k in range(3))
    stack = jnp.concatenate([*thirds(gain), *thirds(delta), about.astype(BF16), jnp.zeros_like(about).astype(BF16)], axis=0)
    lane = lax.broadcasted_iota(jnp.int32, (3 * LANES, 3 * LANES), 1)
    sub = lax.broadcasted_iota(jnp.int32, (3 * LANES, 3 * LANES), 0)
    earlier = jnp.where(sub < lane, 1.0, 0.0).astype(BF16)
    wide = lax.broadcasted_iota(jnp.int32, (LANES, 3 * LANES), 1).astype(F32)
    span = strips // PARTS
    keys = [
        jnp.concatenate(
            [
                reached(n[2], lon_first + h * span, lon_first + (h + 1) * span - 1, lat_first, lat_first + side - 1)
                for n in near
            ],
            axis=1,
        )
        for h in range(PARTS)
    ]
    keys = jnp.concatenate(keys + [jnp.zeros((8 - PARTS, 3 * LANES), F32)], axis=0)
    keys = jnp.concatenate([keys, jnp.zeros_like(keys)], axis=0)
    ahead = jnp.dot(keys.astype(BF16), earlier, preferred_element_type=F32)
    place = lax.broadcasted_iota(jnp.int32, keys.shape, 1).astype(F32)
    ranks = jnp.where(keys > 0.0, ahead, jnp.sum(keys, axis=1, keepdims=True) + place - ahead)
    for h in range(PARTS):
        picks = []
        for i in range(3):
            rank = jnp.broadcast_to(ranks[h : h + 1, i * LANES : (i + 1) * LANES], (LANES, LANES)).T
            picks.append(jnp.where(wide == jnp.concatenate([rank] * 3, axis=1), 1.0, 0.0).astype(BF16))
        moved = jnp.dot(stack, jnp.concatenate(picks, axis=0), preferred_element_type=F32)
        sorted_gain = moved[0:members] + moved[members : 2 * members] + moved[2 * members : 3 * members]
        delta_ref[h] = moved[3 * members : 4 * members] + moved[4 * members : 5 * members] + moved[5 * members : 6 * members]
        about_ref[h] = moved[6 * members : 6 * members + 8]
        for j in range(3):
            part = sorted_gain[:, j * LANES : (j + 1) * LANES]
            part = jnp.concatenate([part, jnp.zeros((LANES - members, LANES), F32)], axis=0)
            both = jnp.concatenate(split(part.T), axis=1)
            w_ref[h * 3 + j, 0:LANES, :] = both
            w_ref[h * 3 + j, LANES:, :] = both

    held = st_ref.reshape(strips * rows, cells)
    lat = lat_first + lax.broadcasted_iota(jnp.int32, (side, 1), 0).astype(F32)

    @pl.loop(0, strips)
    def _(p):
        lon_here = lon_first + p.astype(F32)
        h = p // span
        tapers = []
        for j in range(3):
            facts = about_ref[h, :, j * LANES : (j + 1) * LANES]
            reach = facts[4:5, :]
            gap = jnp.maximum(jnp.abs(lon_here - facts[2:3, :]), jnp.abs(lat - facts[3:4, :]))
            tapers.append(jnp.maximum(0.0, reach - gap) / jnp.maximum(reach, 1.0))

        def matrices(j, first, count):
            delta = delta_ref[h, :, j * LANES : (j + 1) * LANES]
            left = [jnp.concatenate(split(delta * tapers[j][q : q + 1, :]), axis=1) for q in range(first, first + count)]
            both = jnp.dot(jnp.concatenate(left, axis=0), w_ref[h * 3 + j], preferred_element_type=F32)
            return both[:, :LANES] + both[:, LANES:]

        def finish(more):
            for first in range(0, side, GROUP):
                part = pl.ds(first * members, GROUP * members)
                a = matrices(0, first, GROUP)
                high, low = split(a + a_ref[part, :] if more else a)
                left = jnp.concatenate([high[:, :members], high[:, :members], low[:, :members]], axis=1)
                for q in range(0, GROUP, 2):
                    at = [pl.ds(p * rows + first + q + k, members, stride=pitch) for k in range(2)]
                    x = jnp.concatenate([held[at[0], :], held[at[1], :]], axis=1)
                    x_high, x_low = split(x - jnp.sum(x, axis=0, keepdims=True) / members)
                    right = jnp.concatenate([x_high, x_low, x_high], axis=0)
                    change = jnp.dot(left[q * members : (q + 2) * members], right, preferred_element_type=F32)
                    held[at[0], :] = x[:, :cells] + change[:members, :cells]
                    held[at[1], :] = x[:, cells:] + change[members:, cells:]

        far = jnp.max(jnp.maximum(tapers[1], tapers[2])) > 0.0
        copy_in(p).wait()

        @pl.when(far)
        def _():
            for first in range(0, side, GROUP):
                a_ref[pl.ds(first * members, GROUP * members), :] = matrices(1, first, GROUP)

            @pl.when(jnp.max(tapers[2]) > 0.0)
            def _():
                for first in range(0, side, GROUP):
                    a_ref[pl.ds(first * members, GROUP * members), :] += matrices(2, first, GROUP)

            finish(True)

        @pl.when(jnp.logical_not(far))
        def _():
            finish(False)

        copy_out(p).start()

    if points:
        pick(obs, points, side, pitch, members, code_ref, loc_ref, ow_ref, held, sums)
        put_folded(sums, (before_ref, own_ref, after_ref), obs)
    for p in range(strips):
        copy_out(p).wait()


def update(pos, chunks, state, side, obs, following=()):
    members, blocks, cells = state.shape
    strips = blocks // side
    smem = pl.BlockSpec(memory_space=pltpu.SMEM)
    vmem = pl.BlockSpec(memory_space=pltpu.VMEM)
    hbm = pl.BlockSpec(memory_space=pl.ANY)
    rows = jax.ShapeDtypeStruct((3, fold_rows(members, obs), LANES), F32)
    more = 3 if following else 0
    points = following[1].shape[0] // (9 * obs) if following else 0
    out = pl.pallas_call(
        functools.partial(update_kernel, obs, points),
        out_shape=(jax.ShapeDtypeStruct(state.shape, F32),) + (rows,) * more,
        in_specs=[smem] * (1 + more) + [vmem] * 3 + [hbm],
        out_specs=(hbm,) + (vmem,) * more,
        scratch_shapes=[
            pltpu.VMEM((strips, members, pitch_of(side), cells), F32),
            pltpu.VMEM((3 * PARTS, 2 * LANES, 2 * LANES), BF16),
            pltpu.VMEM((PARTS, members, 3 * LANES), F32),
            pltpu.VMEM((PARTS, 8, 3 * LANES), F32),
            pltpu.VMEM((side * members, LANES), F32),
            pltpu.SemaphoreType.DMA((strips,)),
            pltpu.SemaphoreType.DMA((strips,)),
        ]
        + [pltpu.VMEM((3, members, LANES), F32)] * bool(following),
        compiler_params=pltpu.CompilerParams(vmem_limit_bytes=VMEM_LIMIT),
    )(pos, *following, *chunks, state)
    return out


def per_device(prior_state, stencil, weights, obs_values, obs_errors, radius):
    members, side, _, cells = prior_state.shape
    batches, _, _, obs, points = stencil.shape
    lon_index = lax.axis_index("lon")
    lat_index = lax.axis_index("lat")
    lat_total = side * lax.axis_size("lat")
    state = prior_state.reshape(members, side * side, cells)

    own_meta = jnp.concatenate(
        [stencil.reshape(batches, obs * points).astype(F32) + 1.0, weights.reshape(batches, obs * points)]
    )
    first = stencil[:, 0, 0, :, 0]
    about = jnp.stack(
        [
            obs_values[:, 0, 0],
            obs_errors[:, 0, 0],
            (first // (lat_total * cells)).astype(F32),
            (first // cells % lat_total).astype(F32),
            (radius[:, 0, 0] + 1).astype(F32),
        ],
        axis=1,
    )
    about = jnp.pad(about, ((0, 0), (0, 3), (0, LANES - obs)))
    before, after = neighbours(own_meta, "lat")
    row_meta = jnp.concatenate([before, own_meta, after, about.reshape(batches * 8, LANES)])
    before, after = neighbours(row_meta, "lon")
    lon_meta = jnp.stack([before, row_meta, after])
    abouts = lon_meta[:, 3 * 2 * batches :].reshape(3, batches, 8, LANES)
    meta = lon_meta[:, : 3 * 2 * batches].reshape(9, 2, batches, obs * points)
    rows = meta[:, 0].astype(jnp.int32) - 1
    block_lon = rows // (lat_total * cells) - lon_index * side
    block_lat = rows // cells % lat_total - lat_index * side
    here = (rows >= 0) & (block_lon >= 0) & (block_lon < side) & (block_lat >= 0) & (block_lat < side)
    loc = jnp.where(here, (block_lon * side + block_lat) * cells + rows % cells, -1)
    code = jnp.max(here.astype(jnp.int32).reshape(9, batches, obs // WORD, WORD, points), axis=-1)
    code = jnp.sum(code * (1 << jnp.arange(WORD, dtype=jnp.int32)), axis=-1)
    loc = jnp.moveaxis(loc, 1, 0).reshape(batches, -1)
    code = jnp.moveaxis(code, 1, 0).reshape(batches, -1)
    w = jnp.moveaxis(meta[:, 1], 1, 0).reshape(batches, -1)

    pos = jnp.stack([lon_index, lat_index]).astype(jnp.int32)

    means = []
    sums = first_pick(code[0], loc[0], w[0], state, side, obs, points)
    for batch in range(batches):
        to_before, to_own, to_after = sums
        size = lax.axis_size("lat")
        from_before = lax.ppermute(to_after, "lat", [(i, i + 1) for i in range(size - 1)])
        from_after = lax.ppermute(to_before, "lat", [(i + 1, i) for i in range(size - 1)])
        summed = from_before + to_own + from_after
        later = jnp.arange(lax.axis_size("lon"), dtype=jnp.int32)[:, None, None, None] > lon_index
        rows = lax.all_to_all(jnp.where(later, summed[1:], summed[:2]), "lon", 0, 0, tiled=True)
        pack, mean = observe(pos, summed, rows, tuple(abouts[:, batch]), obs, members)
        before, after = neighbours(pack, "lat")
        following = (code[batch + 1], loc[batch + 1], w[batch + 1]) if batch + 1 < batches else ()
        state, *sums = update(pos, (before, pack, after), state, side, obs, following)
        means.append(mean[0, obs : 2 * obs])
    return state.reshape(prior_state.shape), jnp.stack(means)[:, None, None, :]


def solution(mesh):
    placed = (
        P(None, "lon", "lat", None),
        P(None, "lon", "lat", None, None),
        P(None, "lon", "lat", None, None),
        P(None, "lon", "lat", None),
        P(None, "lon", "lat", None),
        P(None, "lon", "lat", None),
    )
    return jax.shard_map(
        per_device,
        mesh=mesh,
        in_specs=placed,
        out_specs=(P(None, "lon", "lat", None), P(None, "lon", "lat", None)),
        check_vma=False,
    )
```

```python
import functools
import jax
import jax.numpy as jnp
from jax import lax
from jax.experimental import pallas as pl
from jax.experimental.pallas import tpu as pltpu
from jax.sharding import PartitionSpec as P

EPS = 1e-06
LANES = 128
WORD = 8
F32 = jnp.float32
BF16 = jnp.bfloat16
VMEM_LIMIT = 48 * 1024 * 1024
UNROLL = 8
GROUP = 16
PARTS = 4


def pitch_of(side):
    return side + 8 if side % 16 == 0 else side


def neighbours(array, axis, distance=1):
    size = lax.axis_size(axis)
    up = [(i, i + distance) for i in range(size - distance)]
    down = [(j, i) for i, j in up]
    return lax.ppermute(array, axis, up), lax.ppermute(array, axis, down)


def split(x):
    high = x.astype(BF16)
    return high, (x - high.astype(F32)).astype(BF16)


def thirds(x):
    high = x.astype(BF16)
    rest = x - high.astype(F32)
    middle = rest.astype(BF16)
    return high, middle, (rest - middle.astype(F32)).astype(BF16)


def placed(x, source, target, obs):
    lane = lax.broadcasted_iota(jnp.int32, (1, LANES), 1)
    shift = (target - source) * obs % LANES
    x = x if shift == 0 else pltpu.roll(x, shift, 1)
    return jnp.where((lane >= target * obs) & (lane < (target + 1) * obs), x, 0.0)


def fold_rows(members, obs):
    return -(-members // (LANES // obs * 8)) * 8


def fold(x, slot, obs):
    members = x.shape[0]
    rows = fold_rows(members, obs)
    x = jnp.concatenate([x, jnp.zeros((LANES // obs * rows - members, LANES), F32)], axis=0)
    return sum(placed(x[k * rows : (k + 1) * rows], slot, k, obs) for k in range(LANES // obs))


def pick(obs, points, side, pitch, members, code_ref, loc_ref, w_ref, held, sums):
    lane = lax.broadcasted_iota(jnp.int32, (members, LANES), 1)
    sums[...] = jnp.zeros_like(sums)

    def one(group, o):
        acc = jnp.zeros((members, LANES), F32)
        for s in range(points):
            at = (group * obs + o) * points + s
            loc = loc_ref[at]
            w = jnp.where(loc >= 0, w_ref[at], 0.0)
            loc = jnp.maximum(loc, 0)
            block = loc // LANES
            start = (block // side) * (members * pitch) + block % side
            x = held[pl.ds(start, members, stride=pitch), :]
            acc = acc + jnp.where(lane == loc % LANES, x * w, 0.0)
        total = jnp.sum(acc, axis=1, keepdims=True)
        return jnp.where(lane == (group // 3) * obs + o, total, 0.0)

    @pl.loop(0, obs // UNROLL)
    def _(t):
        found = [one(4, t * UNROLL + u) for u in range(UNROLL)]
        sums[1] = sums[1] + sum(found[1:], found[0])

    per_group = obs // WORD

    @pl.loop(0, 9 * per_group)
    def _(t):
        word = code_ref[t]

        group = t // per_group

        @pl.when((word > 0) & (group != 4))
        def _():
            def step(left):
                low = left & -left
                bit = sum(((low >> k) > 0).astype(jnp.int32) for k in range(1, WORD))
                sums[group % 3] = sums[group % 3] + one(group, (t % per_group) * WORD + bit)
                return left - low

            lax.while_loop(lambda left: left > 0, step, word)


def put_folded(sums, outs, obs):
    for j, out in enumerate(outs):
        for slot in range(3):
            out[slot] = fold(sums[j], slot, obs)


def strips_in(state_ref, st_ref, side, sem):
    return lambda p: pltpu.make_async_copy(
        state_ref.at[:, pl.ds(p * side, side), :], st_ref.at[p, :, pl.ds(0, side), :], sem.at[p]
    )


def pick_kernel(obs, points, code_ref, loc_ref, w_ref, state_ref, before_ref, own_ref, after_ref, st_ref, sums, sem):
    strips, members, pitch, cells = st_ref.shape
    side = state_ref.shape[1] // strips
    copy = strips_in(state_ref, st_ref, side, sem)
    for p in range(strips):
        copy(p).start()
    for p in range(strips):
        copy(p).wait()
    held = st_ref.reshape(strips * members * pitch, cells)
    pick(obs, points, side, pitch, members, code_ref, loc_ref, w_ref, held, sums)
    put_folded(sums, (before_ref, own_ref, after_ref), obs)


def first_pick(code, loc, w, state, side, obs, points):
    members, blocks, cells = state.shape
    strips = blocks // side
    rows = jax.ShapeDtypeStruct((3, fold_rows(members, obs), LANES), F32)
    smem = pl.BlockSpec(memory_space=pltpu.SMEM)
    vmem = pl.BlockSpec(memory_space=pltpu.VMEM)
    return pl.pallas_call(
        functools.partial(pick_kernel, obs, points),
        out_shape=(rows,) * 3,
        in_specs=[smem, smem, smem, pl.BlockSpec(memory_space=pl.ANY)],
        out_specs=(vmem,) * 3,
        scratch_shapes=[
            pltpu.VMEM((strips, members, pitch_of(side), cells), F32),
            pltpu.VMEM((3, members, LANES), F32),
            pltpu.SemaphoreType.DMA((strips,)),
        ],
        compiler_params=pltpu.CompilerParams(vmem_limit_bytes=VMEM_LIMIT),
    )(code, loc, w, state)


def observe_kernel(obs, members, lon_ref, summed_ref, rows_ref, *refs):
    abouts, (pack_ref, mean_ref) = refs[:3], refs[3:]
    devices = rows_ref.shape[0]

    def sums(distance, slot):
        if distance == 0:
            return summed_ref[slot]
        at = lon_ref[0] + distance
        part = rows_ref[jnp.clip(at, 0, devices - 1), slot - 1 if distance < 0 else slot]
        return jnp.where((at >= 0) & (at < devices), part, 0.0)

    pieces = [0.0] * (LANES // obs)
    about = 0.0
    for t in range(3):
        for slot in range(3):
            part = sums(t - slot, slot)
            pieces = [piece + placed(part, k, t, obs) for k, piece in enumerate(pieces)]
        about = about + placed(abouts[t][...], 0, t, obs)
    ensemble = jnp.concatenate(pieces, axis=0)[:members]
    values = about[0:1, :]
    known = about[4:5, :] > 0.0
    errors = jnp.where(known, about[1:2, :], 1.0)
    mean = jnp.sum(ensemble, axis=0, keepdims=True) / members
    anomaly = ensemble - mean
    spread = jnp.sum(anomaly * anomaly, axis=0, keepdims=True) / (members - 1) + EPS
    post_var = 1.0 / (1.0 / spread + 1.0 / errors)
    post_mean = post_var * (mean / spread + values / errors)
    delta = (post_mean - mean) + (jnp.sqrt(post_var / spread) - 1.0) * anomaly
    gain = anomaly / ((members - 1) * spread)
    pack_ref[0:members, :] = jnp.where(known, gain, 0.0)
    pack_ref[members : 2 * members, :] = jnp.where(known, delta, 0.0)
    pack_ref[2 * members :, :] = about
    mean_ref[...] = jnp.broadcast_to(mean, mean_ref.shape)


def observe(lon, summed, rows, abouts, obs, members):
    vmem = pl.BlockSpec(memory_space=pltpu.VMEM)
    return pl.pallas_call(
        functools.partial(observe_kernel, obs, members),
        out_shape=(
            jax.ShapeDtypeStruct((2 * members + 8, LANES), F32),
            jax.ShapeDtypeStruct((8, LANES), F32),
        ),
        in_specs=[pl.BlockSpec(memory_space=pltpu.SMEM)] + [vmem] * 5,
        out_specs=(vmem, vmem),
    )(lon, summed, rows, *abouts)


def reached(about, lon_first, lon_last, lat_first, lat_last):
    lon, lat, reach = about[2:3, :], about[3:4, :], about[4:5, :]
    lon_gap = jnp.maximum(jnp.maximum(lon_first - lon, lon - lon_last), 0.0)
    lat_gap = jnp.maximum(jnp.maximum(lat_first - lat, lat - lat_last), 0.0)
    return jnp.where(reach > jnp.maximum(lon_gap, lat_gap), 1.0, 0.0)


def update_kernel(obs, points, *refs):
    if points:
        pos_ref, code_ref, loc_ref, ow_ref, c0_ref, c1_ref, c2_ref, state_ref = refs[:8]
        out_ref, before_ref, own_ref, after_ref, sums = refs[8:12] + refs[-1:]
        st_ref, w_ref, delta_ref, about_ref, a_ref, in_sem, out_sem = refs[12:-1]
    else:
        pos_ref, c0_ref, c1_ref, c2_ref, state_ref, out_ref = refs[:6]
        st_ref, w_ref, delta_ref, about_ref, a_ref, in_sem, out_sem = refs[6:]
    strips, members, pitch, cells = st_ref.shape
    side = state_ref.shape[1] // strips
    rows = members * pitch
    copy_in = strips_in(state_ref, st_ref, side, in_sem)

    def copy_out(p):
        return pltpu.make_async_copy(
            st_ref.at[p, :, pl.ds(0, side), :], out_ref.at[:, pl.ds(p * side, side), :], out_sem.at[p]
        )

    for p in range(strips):
        copy_in(p).start()

    lon_first = (pos_ref[0] * side).astype(F32)
    lat_first = (pos_ref[1] * side).astype(F32)
    near = [
        (c[0:members, :], c[members : 2 * members, :], c[2 * members : 2 * members + 8, :])
        for c in (c0_ref, c1_ref, c2_ref)
    ]
    gain, delta, about = (jnp.concatenate([n[k] for n in near], axis=1) for k in range(3))
    stack = jnp.concatenate([*split(gain), *thirds(delta), about.astype(BF16), jnp.zeros_like(about).astype(BF16)], axis=0)
    lane = lax.broadcasted_iota(jnp.int32, (3 * LANES, 3 * LANES), 1)
    sub = lax.broadcasted_iota(jnp.int32, (3 * LANES, 3 * LANES), 0)
    earlier = jnp.where(sub < lane, 1.0, 0.0).astype(BF16)
    span = strips // PARTS
    keys = [
        jnp.concatenate(
            [
                reached(n[2], lon_first + h * span, lon_first + (h + 1) * span - 1, lat_first, lat_first + side - 1)
                for n in near
            ],
            axis=1,
        )
        for h in range(PARTS)
    ]
    keys = jnp.concatenate(keys + [jnp.zeros((8 - PARTS, 3 * LANES), F32)], axis=0)
    keys = jnp.concatenate([keys, jnp.zeros_like(keys)], axis=0)
    ahead = jnp.dot(keys.astype(BF16), earlier, preferred_element_type=F32)
    place = lax.broadcasted_iota(jnp.int32, keys.shape, 1).astype(F32)
    ranks = jnp.where(keys > 0.0, ahead, jnp.sum(keys, axis=1, keepdims=True) + place - ahead)
    counts = jnp.sum(keys, axis=1, keepdims=True)

    def sort(h, first, chunks):
        width = chunks * LANES
        wide = (first * LANES + lax.broadcasted_iota(jnp.int32, (LANES, width), 1)).astype(F32)
        picks = []
        for i in range(3):
            rank = jnp.broadcast_to(ranks[h : h + 1, i * LANES : (i + 1) * LANES], (LANES, LANES)).T
            picks.append(jnp.where(wide == jnp.concatenate([rank] * chunks, axis=1), 1.0, 0.0).astype(BF16))
        moved = jnp.dot(stack, jnp.concatenate(picks, axis=0), preferred_element_type=F32)
        at = 2 * members
        to = slice(first * LANES, first * LANES + width)
        delta_ref[h, :, to] = moved[at : at + members] + moved[at + members : at + 2 * members] + moved[at + 2 * members : at + 3 * members]
        about_ref[h, :, to] = moved[at + 3 * members : at + 3 * members + 8]
        for j in range(chunks):
            both = []
            for k in range(2):
                part = moved[k * members : (k + 1) * members, j * LANES : (j + 1) * LANES]
                part = jnp.concatenate([part, jnp.zeros((LANES - members, LANES), F32)], axis=0)
                both.append(part.T.astype(BF16))
            both = jnp.concatenate(both, axis=1)
            w_ref[h * 3 + first + j, 0:LANES, :] = both
            w_ref[h * 3 + first + j, LANES:, :] = both

    for h in range(PARTS):
        sort(h, 0, 2)
        about_ref[h, :, 2 * LANES :] = jnp.zeros((8, LANES), F32)

    @pl.when(jnp.max(counts) > 2 * LANES)
    def _():
        for h in range(PARTS):
            sort(h, 2, 1)

    held = st_ref.reshape(strips * rows, cells)
    lat = lat_first + lax.broadcasted_iota(jnp.int32, (side, 1), 0).astype(F32)

    @pl.loop(0, strips)
    def _(p):
        lon_here = lon_first + p.astype(F32)
        h = p // span
        tapers = []
        for j in range(3):
            facts = about_ref[h, :, j * LANES : (j + 1) * LANES]
            reach = facts[4:5, :]
            gap = jnp.maximum(jnp.abs(lon_here - facts[2:3, :]), jnp.abs(lat - facts[3:4, :]))
            tapers.append(jnp.maximum(0.0, reach - gap) / jnp.maximum(reach, 1.0))

        def matrices(j, first, count):
            delta = delta_ref[h, :, j * LANES : (j + 1) * LANES]
            left = [jnp.concatenate(split(delta * tapers[j][q : q + 1, :]), axis=1) for q in range(first, first + count)]
            both = jnp.dot(jnp.concatenate(left, axis=0), w_ref[h * 3 + j], preferred_element_type=F32)
            return both[:, :LANES] + both[:, LANES:]

        def finish(more):
            for first in range(0, side, GROUP):
                part = pl.ds(first * members, GROUP * members)
                a = matrices(0, first, GROUP)
                high, low = split(a + a_ref[part, :] if more else a)
                left = jnp.concatenate([high[:, :members], high[:, :members], low[:, :members]], axis=1)
                for q in range(0, GROUP, 2):
                    at = [pl.ds(p * rows + first + q + k, members, stride=pitch) for k in range(2)]
                    x = jnp.concatenate([held[at[0], :], held[at[1], :]], axis=1)
                    x_high, x_low = split(x - jnp.sum(x, axis=0, keepdims=True) / members)
                    right = jnp.concatenate([x_high, x_low, x_high], axis=0)
                    change = jnp.dot(left[q * members : (q + 2) * members], right, preferred_element_type=F32)
                    held[at[0], :] = x[:, :cells] + change[:members, :cells]
                    held[at[1], :] = x[:, cells:] + change[members:, cells:]

        far = jnp.max(jnp.maximum(tapers[1], tapers[2])) > 0.0
        copy_in(p).wait()

        @pl.when(far)
        def _():
            for first in range(0, side, GROUP):
                a_ref[pl.ds(first * members, GROUP * members), :] = matrices(1, first, GROUP)

            @pl.when(jnp.max(tapers[2]) > 0.0)
            def _():
                for first in range(0, side, GROUP):
                    a_ref[pl.ds(first * members, GROUP * members), :] += matrices(2, first, GROUP)

            finish(True)

        @pl.when(jnp.logical_not(far))
        def _():
            finish(False)

        copy_out(p).start()

    if points:
        pick(obs, points, side, pitch, members, code_ref, loc_ref, ow_ref, held, sums)
        put_folded(sums, (before_ref, own_ref, after_ref), obs)
    for p in range(strips):
        copy_out(p).wait()


def update(pos, chunks, state, side, obs, following=()):
    members, blocks, cells = state.shape
    strips = blocks // side
    smem = pl.BlockSpec(memory_space=pltpu.SMEM)
    vmem = pl.BlockSpec(memory_space=pltpu.VMEM)
    hbm = pl.BlockSpec(memory_space=pl.ANY)
    rows = jax.ShapeDtypeStruct((3, fold_rows(members, obs), LANES), F32)
    more = 3 if following else 0
    points = following[1].shape[0] // (9 * obs) if following else 0
    out = pl.pallas_call(
        functools.partial(update_kernel, obs, points),
        out_shape=(jax.ShapeDtypeStruct(state.shape, F32),) + (rows,) * more,
        in_specs=[smem] * (1 + more) + [vmem] * 3 + [hbm],
        out_specs=(hbm,) + (vmem,) * more,
        scratch_shapes=[
            pltpu.VMEM((strips, members, pitch_of(side), cells), F32),
            pltpu.VMEM((3 * PARTS, 2 * LANES, 2 * LANES), BF16),
            pltpu.VMEM((PARTS, members, 3 * LANES), F32),
            pltpu.VMEM((PARTS, 8, 3 * LANES), F32),
            pltpu.VMEM((side * members, LANES), F32),
            pltpu.SemaphoreType.DMA((strips,)),
            pltpu.SemaphoreType.DMA((strips,)),
        ]
        + [pltpu.VMEM((3, members, LANES), F32)] * bool(following),
        compiler_params=pltpu.CompilerParams(vmem_limit_bytes=VMEM_LIMIT),
    )(pos, *following, *chunks, state)
    return out


def per_device(prior_state, stencil, weights, obs_values, obs_errors, radius):
    members, side, _, cells = prior_state.shape
    batches, _, _, obs, points = stencil.shape
    lon_index = lax.axis_index("lon")
    lat_index = lax.axis_index("lat")
    lat_total = side * lax.axis_size("lat")
    state = prior_state.reshape(members, side * side, cells)

    own_meta = jnp.concatenate(
        [stencil.reshape(batches, obs * points).astype(F32) + 1.0, weights.reshape(batches, obs * points)]
    )
    first = stencil[:, 0, 0, :, 0]
    about = jnp.stack(
        [
            obs_values[:, 0, 0],
            obs_errors[:, 0, 0],
            (first // (lat_total * cells)).astype(F32),
            (first // cells % lat_total).astype(F32),
            (radius[:, 0, 0] + 1).astype(F32),
        ],
        axis=1,
    )
    about = jnp.pad(about, ((0, 0), (0, 3), (0, LANES - obs)))
    before, after = neighbours(own_meta, "lat")
    row_meta = jnp.concatenate([before, own_meta, after, about.reshape(batches * 8, LANES)])
    before, after = neighbours(row_meta, "lon")
    lon_meta = jnp.stack([before, row_meta, after])
    abouts = lon_meta[:, 3 * 2 * batches :].reshape(3, batches, 8, LANES)
    meta = lon_meta[:, : 3 * 2 * batches].reshape(9, 2, batches, obs * points)
    rows = meta[:, 0].astype(jnp.int32) - 1
    block_lon = rows // (lat_total * cells) - lon_index * side
    block_lat = rows // cells % lat_total - lat_index * side
    here = (rows >= 0) & (block_lon >= 0) & (block_lon < side) & (block_lat >= 0) & (block_lat < side)
    loc = jnp.where(here, (block_lon * side + block_lat) * cells + rows % cells, -1)
    code = jnp.max(here.astype(jnp.int32).reshape(9, batches, obs // WORD, WORD, points), axis=-1)
    code = jnp.sum(code * (1 << jnp.arange(WORD, dtype=jnp.int32)), axis=-1)
    loc = jnp.moveaxis(loc, 1, 0).reshape(batches, -1)
    code = jnp.moveaxis(code, 1, 0).reshape(batches, -1)
    w = jnp.moveaxis(meta[:, 1], 1, 0).reshape(batches, -1)

    pos = jnp.stack([lon_index, lat_index]).astype(jnp.int32)

    means = []
    sums = first_pick(code[0], loc[0], w[0], state, side, obs, points)
    for batch in range(batches):
        to_before, to_own, to_after = sums
        size = lax.axis_size("lat")
        from_before = lax.ppermute(to_after, "lat", [(i, i + 1) for i in range(size - 1)])
        from_after = lax.ppermute(to_before, "lat", [(i + 1, i) for i in range(size - 1)])
        summed = from_before + to_own + from_after
        later = jnp.arange(lax.axis_size("lon"), dtype=jnp.int32)[:, None, None, None] > lon_index
        rows = lax.all_to_all(jnp.where(later, summed[1:], summed[:2]), "lon", 0, 0, tiled=True)
        pack, mean = observe(pos, summed, rows, tuple(abouts[:, batch]), obs, members)
        before, after = neighbours(pack, "lat")
        following = (code[batch + 1], loc[batch + 1], w[batch + 1]) if batch + 1 < batches else ()
        state, *sums = update(pos, (before, pack, after), state, side, obs, following)
        means.append(mean[0, obs : 2 * obs])
    return state.reshape(prior_state.shape), jnp.stack(means)[:, None, None, :]


def solution(mesh):
    placed = (
        P(None, "lon", "lat", None),
        P(None, "lon", "lat", None, None),
        P(None, "lon", "lat", None, None),
        P(None, "lon", "lat", None),
        P(None, "lon", "lat", None),
        P(None, "lon", "lat", None),
    )
    return jax.shard_map(
        per_device,
        mesh=mesh,
        in_specs=placed,
        out_specs=(P(None, "lon", "lat", None), P(None, "lon", "lat", None)),
        check_vma=False,
    )
```

```python
import functools
import jax
import jax.numpy as jnp
from jax import lax
from jax.experimental import pallas as pl
from jax.experimental.pallas import tpu as pltpu
from jax.sharding import PartitionSpec as P

EPS = 1e-06
LANES = 128
WORD = 16
F32 = jnp.float32
BF16 = jnp.bfloat16
VMEM_LIMIT = 48 * 1024 * 1024
UNROLL = 16
GROUP = 16
PARTS = 4


def pitch_of(side):
    return side + 8 if side % 16 == 0 else side


def neighbours(array, axis, distance=1):
    size = lax.axis_size(axis)
    up = [(i, i + distance) for i in range(size - distance)]
    down = [(j, i) for i, j in up]
    return lax.ppermute(array, axis, up), lax.ppermute(array, axis, down)


def split(x):
    high = x.astype(BF16)
    return high, (x - high.astype(F32)).astype(BF16)


def thirds(x):
    high = x.astype(BF16)
    rest = x - high.astype(F32)
    middle = rest.astype(BF16)
    return high, middle, (rest - middle.astype(F32)).astype(BF16)


def placed(x, source, target, obs):
    lane = lax.broadcasted_iota(jnp.int32, (1, LANES), 1)
    shift = (target - source) * obs % LANES
    x = x if shift == 0 else pltpu.roll(x, shift, 1)
    return jnp.where((lane >= target * obs) & (lane < (target + 1) * obs), x, 0.0)


def fold_rows(members, obs):
    return -(-members // (LANES // obs * 8)) * 8


def fold(x, slot, obs):
    members = x.shape[0]
    rows = fold_rows(members, obs)
    x = jnp.concatenate([x, jnp.zeros((LANES // obs * rows - members, LANES), F32)], axis=0)
    return sum(placed(x[k * rows : (k + 1) * rows], slot, k, obs) for k in range(LANES // obs))


def pick(obs, points, side, pitch, members, code_ref, loc_ref, w_ref, held, sums):
    lane = lax.broadcasted_iota(jnp.int32, (members, LANES), 1)
    sums[...] = jnp.zeros_like(sums)

    def one(group, o):
        acc = jnp.zeros((members, LANES), F32)
        for s in range(points):
            at = (group * obs + o) * points + s
            loc = loc_ref[at]
            w = jnp.where(loc >= 0, w_ref[at], 0.0)
            loc = jnp.maximum(loc, 0)
            block = loc // LANES
            start = (block // side) * (members * pitch) + block % side
            x = held[pl.ds(start, members, stride=pitch), :]
            acc = acc + jnp.where(lane == loc % LANES, x * w, 0.0)
        total = jnp.sum(acc, axis=1, keepdims=True)
        return jnp.where(lane == (group // 3) * obs + o, total, 0.0)

    @pl.loop(0, obs // UNROLL)
    def _(t):
        found = [one(4, t * UNROLL + u) for u in range(UNROLL)]
        sums[1] = sums[1] + sum(found[1:], found[0])

    per_group = obs // WORD

    @pl.loop(0, 9 * per_group)
    def _(t):
        word = code_ref[t]

        group = t // per_group

        @pl.when((word > 0) & (group != 4))
        def _():
            def step(left):
                low = left & -left
                bit = sum(((low >> k) > 0).astype(jnp.int32) for k in range(1, WORD))
                sums[group % 3] = sums[group % 3] + one(group, (t % per_group) * WORD + bit)
                return left - low

            lax.while_loop(lambda left: left > 0, step, word)


def put_folded(sums, outs, obs):
    for j, out in enumerate(outs):
        for slot in range(3):
            out[slot] = fold(sums[j], slot, obs)


def strips_in(state_ref, st_ref, side, sem):
    return lambda p: pltpu.make_async_copy(
        state_ref.at[:, pl.ds(p * side, side), :], st_ref.at[p, :, pl.ds(0, side), :], sem.at[p]
    )


def pick_kernel(obs, points, code_ref, loc_ref, w_ref, state_ref, before_ref, own_ref, after_ref, st_ref, sums, sem):
    strips, members, pitch, cells = st_ref.shape
    side = state_ref.shape[1] // strips
    copy = strips_in(state_ref, st_ref, side, sem)
    for p in range(strips):
        copy(p).start()
    for p in range(strips):
        copy(p).wait()
    held = st_ref.reshape(strips * members * pitch, cells)
    pick(obs, points, side, pitch, members, code_ref, loc_ref, w_ref, held, sums)
    put_folded(sums, (before_ref, own_ref, after_ref), obs)


def first_pick(code, loc, w, state, side, obs, points):
    members, blocks, cells = state.shape
    strips = blocks // side
    rows = jax.ShapeDtypeStruct((3, fold_rows(members, obs), LANES), F32)
    smem = pl.BlockSpec(memory_space=pltpu.SMEM)
    vmem = pl.BlockSpec(memory_space=pltpu.VMEM)
    return pl.pallas_call(
        functools.partial(pick_kernel, obs, points),
        out_shape=(rows,) * 3,
        in_specs=[smem, smem, smem, pl.BlockSpec(memory_space=pl.ANY)],
        out_specs=(vmem,) * 3,
        scratch_shapes=[
            pltpu.VMEM((strips, members, pitch_of(side), cells), F32),
            pltpu.VMEM((3, members, LANES), F32),
            pltpu.SemaphoreType.DMA((strips,)),
        ],
        compiler_params=pltpu.CompilerParams(vmem_limit_bytes=VMEM_LIMIT),
    )(code, loc, w, state)


def observe_kernel(obs, members, lon_ref, summed_ref, rows_ref, *refs):
    abouts, (pack_ref, mean_ref) = refs[:3], refs[3:]
    devices = rows_ref.shape[0]

    def sums(distance, slot):
        if distance == 0:
            return summed_ref[slot]
        at = lon_ref[0] + distance
        part = rows_ref[jnp.clip(at, 0, devices - 1), slot - 1 if distance < 0 else slot]
        return jnp.where((at >= 0) & (at < devices), part, 0.0)

    pieces = [0.0] * (LANES // obs)
    about = 0.0
    for t in range(3):
        for slot in range(3):
            part = sums(t - slot, slot)
            pieces = [piece + placed(part, k, t, obs) for k, piece in enumerate(pieces)]
        about = about + placed(abouts[t][...], 0, t, obs)
    ensemble = jnp.concatenate(pieces, axis=0)[:members]
    values = about[0:1, :]
    known = about[4:5, :] > 0.0
    errors = jnp.where(known, about[1:2, :], 1.0)
    mean = jnp.sum(ensemble, axis=0, keepdims=True) / members
    anomaly = ensemble - mean
    spread = jnp.sum(anomaly * anomaly, axis=0, keepdims=True) / (members - 1) + EPS
    post_var = 1.0 / (1.0 / spread + 1.0 / errors)
    post_mean = post_var * (mean / spread + values / errors)
    delta = (post_mean - mean) + (jnp.sqrt(post_var / spread) - 1.0) * anomaly
    gain = anomaly / ((members - 1) * spread)
    pack_ref[0:members, :] = jnp.where(known, gain, 0.0)
    pack_ref[members : 2 * members, :] = jnp.where(known, delta, 0.0)
    pack_ref[2 * members :, :] = about
    mean_ref[...] = jnp.broadcast_to(mean, mean_ref.shape)


def observe(lon, summed, rows, abouts, obs, members):
    vmem = pl.BlockSpec(memory_space=pltpu.VMEM)
    return pl.pallas_call(
        functools.partial(observe_kernel, obs, members),
        out_shape=(
            jax.ShapeDtypeStruct((2 * members + 8, LANES), F32),
            jax.ShapeDtypeStruct((8, LANES), F32),
        ),
        in_specs=[pl.BlockSpec(memory_space=pltpu.SMEM)] + [vmem] * 5,
        out_specs=(vmem, vmem),
    )(lon, summed, rows, *abouts)


def reached(about, lon_first, lon_last, lat_first, lat_last):
    lon, lat, reach = about[2:3, :], about[3:4, :], about[4:5, :]
    lon_gap = jnp.maximum(jnp.maximum(lon_first - lon, lon - lon_last), 0.0)
    lat_gap = jnp.maximum(jnp.maximum(lat_first - lat, lat - lat_last), 0.0)
    return jnp.where(reach > jnp.maximum(lon_gap, lat_gap), 1.0, 0.0)


def update_kernel(obs, points, *refs):
    if points:
        pos_ref, code_ref, loc_ref, ow_ref, c0_ref, c1_ref, c2_ref, state_ref = refs[:8]
        out_ref, before_ref, own_ref, after_ref, sums = refs[8:12] + refs[-1:]
        st_ref, w_ref, delta_ref, about_ref, a_ref, in_sem, out_sem = refs[12:-1]
    else:
        pos_ref, c0_ref, c1_ref, c2_ref, state_ref, out_ref = refs[:6]
        st_ref, w_ref, delta_ref, about_ref, a_ref, in_sem, out_sem = refs[6:]
    strips, members, pitch, cells = st_ref.shape
    side = state_ref.shape[1] // strips
    rows = members * pitch
    copy_in = strips_in(state_ref, st_ref, side, in_sem)

    def copy_out(p):
        return pltpu.make_async_copy(
            st_ref.at[p, :, pl.ds(0, side), :], out_ref.at[:, pl.ds(p * side, side), :], out_sem.at[p]
        )

    for p in range(strips):
        copy_in(p).start()

    lon_first = (pos_ref[0] * side).astype(F32)
    lat_first = (pos_ref[1] * side).astype(F32)
    near = [
        (c[0:members, :], c[members : 2 * members, :], c[2 * members : 2 * members + 8, :])
        for c in (c0_ref, c1_ref, c2_ref)
    ]
    gain, delta, about = (jnp.concatenate([n[k] for n in near], axis=1) for k in range(3))
    stack = jnp.concatenate([*split(gain), *thirds(delta), about.astype(BF16), jnp.zeros_like(about).astype(BF16)], axis=0)
    lane = lax.broadcasted_iota(jnp.int32, (3 * LANES, 3 * LANES), 1)
    sub = lax.broadcasted_iota(jnp.int32, (3 * LANES, 3 * LANES), 0)
    earlier = jnp.where(sub < lane, 1.0, 0.0).astype(BF16)
    span = strips // PARTS
    keys = [
        jnp.concatenate(
            [
                reached(n[2], lon_first + h * span, lon_first + (h + 1) * span - 1, lat_first, lat_first + side - 1)
                for n in near
            ],
            axis=1,
        )
        for h in range(PARTS)
    ]
    keys = jnp.concatenate(keys + [jnp.zeros((8 - PARTS, 3 * LANES), F32)], axis=0)
    keys = jnp.concatenate([keys, jnp.zeros_like(keys)], axis=0)
    ahead = jnp.dot(keys.astype(BF16), earlier, preferred_element_type=F32)
    place = lax.broadcasted_iota(jnp.int32, keys.shape, 1).astype(F32)
    ranks = jnp.where(keys > 0.0, ahead, jnp.sum(keys, axis=1, keepdims=True) + place - ahead)
    counts = jnp.sum(keys, axis=1, keepdims=True)

    def sort(h, first, chunks):
        width = chunks * LANES
        wide = (first * LANES + lax.broadcasted_iota(jnp.int32, (LANES, width), 1)).astype(F32)
        picks = []
        for i in range(3):
            rank = jnp.broadcast_to(ranks[h : h + 1, i * LANES : (i + 1) * LANES], (LANES, LANES)).T
            picks.append(jnp.where(wide == jnp.concatenate([rank] * chunks, axis=1), 1.0, 0.0).astype(BF16))
        moved = jnp.dot(stack, jnp.concatenate(picks, axis=0), preferred_element_type=F32)
        at = 2 * members
        to = slice(first * LANES, first * LANES + width)
        delta_ref[h, :, to] = moved[at : at + members] + moved[at + members : at + 2 * members] + moved[at + 2 * members : at + 3 * members]
        about_ref[h, :, to] = moved[at + 3 * members : at + 3 * members + 8]
        for j in range(chunks):
            both = []
            for k in range(2):
                part = moved[k * members : (k + 1) * members, j * LANES : (j + 1) * LANES]
                part = jnp.concatenate([part, jnp.zeros((LANES - members, LANES), F32)], axis=0)
                both.append(part.T.astype(BF16))
            both = jnp.concatenate(both, axis=1)
            w_ref[h * 3 + first + j, 0:LANES, :] = both
            w_ref[h * 3 + first + j, LANES:, :] = both

    for h in range(PARTS):
        sort(h, 0, 2)
        about_ref[h, :, 2 * LANES :] = jnp.zeros((8, LANES), F32)

    @pl.when(jnp.max(counts) > 2 * LANES)
    def _():
        for h in range(PARTS):
            sort(h, 2, 1)

    held = st_ref.reshape(strips * rows, cells)
    lat = lat_first + lax.broadcasted_iota(jnp.int32, (side, 1), 0).astype(F32)

    @pl.loop(0, strips)
    def _(p):
        lon_here = lon_first + p.astype(F32)
        h = p // span
        tapers = []
        for j in range(3):
            facts = about_ref[h, :, j * LANES : (j + 1) * LANES]
            reach = facts[4:5, :]
            gap = jnp.maximum(jnp.abs(lon_here - facts[2:3, :]), jnp.abs(lat - facts[3:4, :]))
            tapers.append(jnp.maximum(0.0, reach - gap) / jnp.maximum(reach, 1.0))

        def matrices(j, first, count):
            delta = delta_ref[h, :, j * LANES : (j + 1) * LANES]
            left = [jnp.concatenate(split(delta * tapers[j][q : q + 1, :]), axis=1) for q in range(first, first + count)]
            both = jnp.dot(jnp.concatenate(left, axis=0), w_ref[h * 3 + j], preferred_element_type=F32)
            return both[:, :LANES] + both[:, LANES:]

        def finish(more):
            for first in range(0, side, GROUP):
                part = pl.ds(first * members, GROUP * members)
                a = matrices(0, first, GROUP)
                high, low = split(a + a_ref[part, :] if more else a)
                left = jnp.concatenate([high[:, :members], high[:, :members], low[:, :members]], axis=1)
                for q in range(0, GROUP, 2):
                    at = [pl.ds(p * rows + first + q + k, members, stride=pitch) for k in range(2)]
                    x = jnp.concatenate([held[at[0], :], held[at[1], :]], axis=1)
                    x_high, x_low = split(x - jnp.sum(x, axis=0, keepdims=True) / members)
                    right = jnp.concatenate([x_high, x_low, x_high], axis=0)
                    change = jnp.dot(left[q * members : (q + 2) * members], right, preferred_element_type=F32)
                    held[at[0], :] = x[:, :cells] + change[:members, :cells]
                    held[at[1], :] = x[:, cells:] + change[members:, cells:]

        far = jnp.max(jnp.maximum(tapers[1], tapers[2])) > 0.0
        copy_in(p).wait()

        @pl.when(far)
        def _():
            for first in range(0, side, GROUP):
                a_ref[pl.ds(first * members, GROUP * members), :] = matrices(1, first, GROUP)

            @pl.when(jnp.max(tapers[2]) > 0.0)
            def _():
                for first in range(0, side, GROUP):
                    a_ref[pl.ds(first * members, GROUP * members), :] += matrices(2, first, GROUP)

            finish(True)

        @pl.when(jnp.logical_not(far))
        def _():
            finish(False)

        copy_out(p).start()

    if points:
        pick(obs, points, side, pitch, members, code_ref, loc_ref, ow_ref, held, sums)
        put_folded(sums, (before_ref, own_ref, after_ref), obs)
    for p in range(strips):
        copy_out(p).wait()


def update(pos, chunks, state, side, obs, following=()):
    members, blocks, cells = state.shape
    strips = blocks // side
    smem = pl.BlockSpec(memory_space=pltpu.SMEM)
    vmem = pl.BlockSpec(memory_space=pltpu.VMEM)
    hbm = pl.BlockSpec(memory_space=pl.ANY)
    rows = jax.ShapeDtypeStruct((3, fold_rows(members, obs), LANES), F32)
    more = 3 if following else 0
    points = following[1].shape[0] // (9 * obs) if following else 0
    out = pl.pallas_call(
        functools.partial(update_kernel, obs, points),
        out_shape=(jax.ShapeDtypeStruct(state.shape, F32),) + (rows,) * more,
        in_specs=[smem] * (1 + more) + [vmem] * 3 + [hbm],
        out_specs=(hbm,) + (vmem,) * more,
        scratch_shapes=[
            pltpu.VMEM((strips, members, pitch_of(side), cells), F32),
            pltpu.VMEM((3 * PARTS, 2 * LANES, 2 * LANES), BF16),
            pltpu.VMEM((PARTS, members, 3 * LANES), F32),
            pltpu.VMEM((PARTS, 8, 3 * LANES), F32),
            pltpu.VMEM((side * members, LANES), F32),
            pltpu.SemaphoreType.DMA((strips,)),
            pltpu.SemaphoreType.DMA((strips,)),
        ]
        + [pltpu.VMEM((3, members, LANES), F32)] * bool(following),
        compiler_params=pltpu.CompilerParams(vmem_limit_bytes=VMEM_LIMIT),
    )(pos, *following, *chunks, state)
    return out


def per_device(prior_state, stencil, weights, obs_values, obs_errors, radius):
    members, side, _, cells = prior_state.shape
    batches, _, _, obs, points = stencil.shape
    lon_index = lax.axis_index("lon")
    lat_index = lax.axis_index("lat")
    lat_total = side * lax.axis_size("lat")
    state = prior_state.reshape(members, side * side, cells)

    own_meta = jnp.concatenate(
        [stencil.reshape(batches, obs * points).astype(F32) + 1.0, weights.reshape(batches, obs * points)]
    )
    first = stencil[:, 0, 0, :, 0]
    about = jnp.stack(
        [
            obs_values[:, 0, 0],
            obs_errors[:, 0, 0],
            (first // (lat_total * cells)).astype(F32),
            (first // cells % lat_total).astype(F32),
            (radius[:, 0, 0] + 1).astype(F32),
        ],
        axis=1,
    )
    about = jnp.pad(about, ((0, 0), (0, 3), (0, LANES - obs)))
    before, after = neighbours(own_meta, "lat")
    row_meta = jnp.concatenate([before, own_meta, after, about.reshape(batches * 8, LANES)])
    before, after = neighbours(row_meta, "lon")
    lon_meta = jnp.stack([before, row_meta, after])
    abouts = lon_meta[:, 3 * 2 * batches :].reshape(3, batches, 8, LANES)
    meta = lon_meta[:, : 3 * 2 * batches].reshape(9, 2, batches, obs * points)
    rows = meta[:, 0].astype(jnp.int32) - 1
    block_lon = rows // (lat_total * cells) - lon_index * side
    block_lat = rows // cells % lat_total - lat_index * side
    here = (rows >= 0) & (block_lon >= 0) & (block_lon < side) & (block_lat >= 0) & (block_lat < side)
    loc = jnp.where(here, (block_lon * side + block_lat) * cells + rows % cells, -1)
    code = jnp.max(here.astype(jnp.int32).reshape(9, batches, obs // WORD, WORD, points), axis=-1)
    code = jnp.sum(code * (1 << jnp.arange(WORD, dtype=jnp.int32)), axis=-1)
    loc = jnp.moveaxis(loc, 1, 0).reshape(batches, -1)
    code = jnp.moveaxis(code, 1, 0).reshape(batches, -1)
    w = jnp.moveaxis(meta[:, 1], 1, 0).reshape(batches, -1)

    pos = jnp.stack([lon_index, lat_index]).astype(jnp.int32)

    means = []
    sums = first_pick(code[0], loc[0], w[0], state, side, obs, points)
    for batch in range(batches):
        to_before, to_own, to_after = sums
        size = lax.axis_size("lat")
        from_before = lax.ppermute(to_after, "lat", [(i, i + 1) for i in range(size - 1)])
        from_after = lax.ppermute(to_before, "lat", [(i + 1, i) for i in range(size - 1)])
        summed = from_before + to_own + from_after
        later = jnp.arange(lax.axis_size("lon"), dtype=jnp.int32)[:, None, None, None] > lon_index
        rows = lax.all_to_all(jnp.where(later, summed[1:], summed[:2]), "lon", 0, 0, tiled=True)
        pack, mean = observe(pos, summed, rows, tuple(abouts[:, batch]), obs, members)
        before, after = neighbours(pack, "lat")
        following = (code[batch + 1], loc[batch + 1], w[batch + 1]) if batch + 1 < batches else ()
        state, *sums = update(pos, (before, pack, after), state, side, obs, following)
        means.append(mean[0, obs : 2 * obs])
    return state.reshape(prior_state.shape), jnp.stack(means)[:, None, None, :]


def solution(mesh):
    placed = (
        P(None, "lon", "lat", None),
        P(None, "lon", "lat", None, None),
        P(None, "lon", "lat", None, None),
        P(None, "lon", "lat", None),
        P(None, "lon", "lat", None),
        P(None, "lon", "lat", None),
    )
    return jax.shard_map(
        per_device,
        mesh=mesh,
        in_specs=placed,
        out_specs=(P(None, "lon", "lat", None), P(None, "lon", "lat", None)),
        check_vma=False,
    )
```
